32 devices in a mesh: groups: 2 (over y), rows: 16 (over z, x, core).
Axes of the slice: x: 2, y: 2, z: 4, core: 2. Of those that a mesh axis runs over, the one named last changes fastest.
Arguments:
- charges: bfloat16 [32768, 64], P(('groups', 'rows')), parts along dimension 0, may hold values from -6 to 6
- targets: bfloat16 [32768, 64], P(('groups', 'rows')), parts along dimension 0, may hold values from -6 to 6
- panel_order: int32 [32, 1024], P(('groups', 'rows')), parts along dimension 0, may hold values from 0 to 1023, each once within a row
- near_blocks: bfloat16 [2048, 128, 128], P(('groups', 'rows')), parts along dimension 0, may hold values from -0.1875 to 0.1875
- near_rows: int32 [2048], P(('groups', 'rows')), parts along dimension 0, may hold values from 0 to 7
- near_cols: int32 [2048], P(('groups', 'rows')), parts along dimension 0, may hold values from 0 to 9
- far_left: bfloat16 [512, 128, 32], P(('groups', 'rows')), parts along dimension 0, may hold values from -0.75 to 0.75
- far_right: bfloat16 [512, 128, 32], P(('groups', 'rows')), parts along dimension 0, may hold values from -0.5 to 0.5
- far_rows: int32 [512], P(('groups', 'rows')), parts along dimension 0, may hold values from 0 to 7
- far_slot: int32 [512], P(('groups', 'rows')), parts along dimension 0, may hold values from 0 to 63, as said below
- far_table: int32 [32, 64], P(('groups', 'rows')), parts along dimension 0, may hold values from -1 to 7, as said below
Outputs:
- potentials: bfloat16 [32768, 64], P(('groups', 'rows')), parts along dimension 0
- gradient: float32 [32768, 64], P(('groups', 'rows')), parts along dimension 0
The draws below stay inside these ranges and needn't reach their ends.
There are 2 independent parts, one for each index of `groups`. The reference program is written for one: setup_inputs(seed, part) draws one part's arguments, and reference() takes and returns one part's arrays. A program takes and returns all parts, laid end to end along the dimension named above; each array names one. Nothing has to cross between parts.
Inputs may be any that keep to these rules, and one draw needn't show every extreme that they name: Per device, far_slot values are distinct; of the 16 far blocks of one device, 2 column owners hold 4 each, 2 hold two, 4 hold one and the rest none. far_table[s, t * 4 + k] is the local column cluster of device t's far block with slot s * 4 + k, and -1 exactly where device t has no such block.
All inputs are finite; a program needn't handle non-finite values.
Results may differ from the reference program's by a relative error of at most 0.0044.
Values may be sent and summed in bfloat16 or wider, within the bound.
A program may use at most 128 MiB of HBM per device.

```python
import jax
import jax.numpy as jnp
from jax import lax

LEAF = 128
EXC = 64
RANK = 32
CAP = 4
NEAR_PER = 8
CL_DEV = 8
PAN_DEV = 1024
PANELS = 16384
NEAR_DEV = 64
NEARS = 1024
FAR_DEV = 16
FARS = 256
N_ROWS = 16


def far_plan(key):
    pair_key, column_key, shuffle_key = jax.random.split(key, 3)
    pairs = jax.vmap(lambda part_key: jax.random.permutation(part_key, N_ROWS))(jax.random.split(pair_key, N_ROWS)).astype(jnp.int32)
    leading = pairs[0]
    top_place = jnp.argmax(leading == N_ROWS - 1)
    leading = leading.at[top_place].set(leading[0]).at[0].set(N_ROWS - 1)
    pairs = pairs.at[0].set(leading)
    eighth = N_ROWS // 8
    blocks = jnp.arange(N_ROWS, dtype=jnp.int32)
    heavy = blocks < CAP * eighth
    middle = (blocks >= CAP * eighth) & (blocks < (CAP + 2) * eighth)
    rest_start = (CAP + 2) * eighth
    position = jnp.where(heavy, blocks // CAP, jnp.where(middle, eighth + (blocks - CAP * eighth) // 2, 2 * eighth + blocks - rest_start))
    within = jnp.where(heavy, blocks % CAP, jnp.where(middle, (blocks - CAP * eighth) % 2, 0))
    chosen_pairs = jnp.take_along_axis(pairs, jnp.broadcast_to(position[None, :], (N_ROWS, N_ROWS)), axis=1)
    slot_grid = chosen_pairs * CAP + within[None, :]
    shuffle = jax.vmap(lambda part_key: jax.random.permutation(part_key, N_ROWS))(jax.random.split(shuffle_key, N_ROWS)).astype(jnp.int32)
    slot_grid = jnp.take_along_axis(slot_grid, shuffle, axis=1)
    columns = jax.random.randint(column_key, (N_ROWS, N_ROWS), 0, CL_DEV, dtype=jnp.int32)
    columns = columns.at[0, 0].set(CL_DEV - 1)
    owners = jnp.broadcast_to(jnp.arange(N_ROWS, dtype=jnp.int32)[:, None], (N_ROWS, N_ROWS))
    table = jnp.full((N_ROWS, N_ROWS * CAP), -1, jnp.int32).at[owners, slot_grid].set(columns)
    table = table.reshape(N_ROWS, N_ROWS, CAP).transpose(1, 0, 2).reshape(N_ROWS, N_ROWS * CAP)
    return (slot_grid.reshape(-1), table)


def draw_far_slot(key, part):
    return far_plan(key)[0]


def draw_far_table(key, part):
    return far_plan(key)[1]


def place_ends(drawn, rng, least, top_value):
    spot = [jax.random.randint(jax.random.fold_in(rng, axis), (), 0, length) for axis, length in enumerate(drawn.shape)]
    widest = drawn.shape.index(max(drawn.shape))
    next_to = spot[:widest] + [(spot[widest] + 1) % drawn.shape[widest]] + spot[widest + 1:]
    return drawn.at[tuple(spot)].set(least).at[tuple(next_to)].set(top_value)


def level_of(own_key, dims, cuts, smallest, high):
    factor_of = 1.0
    for dim, blocks in cuts:
        heights = jax.random.uniform(jax.random.fold_in(jax.random.fold_in(own_key, 6), dim), (blocks,), jnp.float32, smallest / len(cuts), high / len(cuts))
        factor_of = factor_of * jnp.repeat(jnp.exp(heights), dims[dim] // blocks).reshape((-1,) + (1,) * (len(dims) - 1 - dim))
    return factor_of


def normal_values(own_key, extent, deviation, bound, cuts=(), kind=jnp.bfloat16):
    entries = jax.random.normal(own_key, extent, jnp.float32) * deviation
    if len(cuts) > 0:
        entries = level_of(own_key, extent, cuts, -0.22, 0.18) * entries
    return jnp.clip(entries, min=-bound, max=bound).astype(kind)


def setup_inputs(seed: int = 0, part: int = 0) -> dict:
    key_of = jax.random.split(jax.random.key(seed), 12)
    part_splits = jax.random.split(jax.random.fold_in(key_of[11], part), 12)
    return {
        "charges": normal_values(part_splits[0], (PANELS, EXC), 1.0, 6.0, ((0, 16),)),
        "targets": normal_values(part_splits[1], (PANELS, EXC), 1.0, 6.0, ((0, 16),)),
        "panel_order": jax.vmap(lambda own: jax.random.permutation(own, PAN_DEV))(jax.random.split(part_splits[2], N_ROWS)).reshape((N_ROWS, PAN_DEV)).astype(jnp.int32),
        "near_blocks": normal_values(part_splits[3], (NEARS, LEAF, LEAF), (LEAF * NEAR_PER) ** -0.5, 0.1875, ((0, 16),)),
        "near_rows": place_ends(jax.random.randint(part_splits[4], (NEARS,), 0, CL_DEV), jax.random.fold_in(part_splits[4], 1), 0, CL_DEV - 1).astype(jnp.int32),
        "near_cols": place_ends(jax.random.randint(part_splits[5], (NEARS,), 0, CL_DEV + 2), jax.random.fold_in(part_splits[5], 1), 0, (CL_DEV + 2) - 1).astype(jnp.int32),
        "far_left": normal_values(part_splits[6], (FARS, LEAF, RANK), (RANK * N_ROWS // CL_DEV) ** -0.5, 0.75, ((0, 16),)),
        "far_right": normal_values(part_splits[7], (FARS, LEAF, RANK), LEAF ** -0.5, 0.5, ((0, 16),)),
        "far_rows": place_ends(jax.random.randint(part_splits[8], (FARS,), 0, CL_DEV), jax.random.fold_in(part_splits[8], 1), 0, CL_DEV - 1).astype(jnp.int32),
        "far_slot": draw_far_slot(jax.random.fold_in(jax.random.fold_in(key_of[11], part), 71), part),
        "far_table": draw_far_table(jax.random.fold_in(jax.random.fold_in(key_of[11], part), 71), part),
    }


def reference(charges, targets, panel_order, near_blocks, near_rows, near_cols, far_left, far_right, far_rows, far_slot, far_table):
    pan_dev = CL_DEV * LEAF
    cluster_total = CL_DEV * N_ROWS
    base_rows = (jnp.arange(N_ROWS, dtype=jnp.int32) * pan_dev)[:, None]
    panel_index = (base_rows + panel_order).reshape(-1).astype(jnp.int32)
    ordered = charges[panel_index].reshape(cluster_total, LEAF, EXC)
    wanted = targets[panel_index].astype(jnp.float32).reshape(cluster_total, LEAF, EXC)
    zero_block = jnp.zeros((1, LEAF, EXC), jnp.bfloat16)
    padded = jnp.concatenate([zero_block, ordered, zero_block], axis=0)

    def far_columns(device, slot_vals):
        source = slot_vals // CAP
        place = slot_vals % CAP
        local = far_table[source, device * CAP + place]
        return (source * CL_DEV + local).astype(jnp.int32)

    def forward_device(device):
        blocks = lax.dynamic_slice_in_dim(near_blocks, device * NEAR_DEV, NEAR_DEV).astype(jnp.float32)
        rows_here = lax.dynamic_slice_in_dim(near_rows, device * NEAR_DEV, NEAR_DEV)
        cols_here = lax.dynamic_slice_in_dim(near_cols, device * NEAR_DEV, NEAR_DEV)
        near_in = padded[(device * CL_DEV + cols_here).astype(jnp.int32)].astype(jnp.float32)
        near_out = jnp.einsum("bij,bje->bie", blocks, near_in)
        field = jnp.zeros((CL_DEV, LEAF, EXC), jnp.float32).at[rows_here].add(near_out)
        left = lax.dynamic_slice_in_dim(far_left, device * FAR_DEV, FAR_DEV).astype(jnp.float32)
        right = lax.dynamic_slice_in_dim(far_right, device * FAR_DEV, FAR_DEV).astype(jnp.float32)
        frows = lax.dynamic_slice_in_dim(far_rows, device * FAR_DEV, FAR_DEV)
        fslot = lax.dynamic_slice_in_dim(far_slot, device * FAR_DEV, FAR_DEV)
        far_in = ordered[far_columns(device, fslot)].astype(jnp.float32)
        coef = jnp.einsum("bir,bie->bre", right, far_in).astype(jnp.bfloat16)
        far_out = jnp.einsum("bir,bre->bie", left, coef.astype(jnp.float32))
        return field.at[frows].add(far_out)

    field = lax.map(forward_device, jnp.arange(N_ROWS, dtype=jnp.int32)).reshape(cluster_total, LEAF, EXC)
    misfit = (field - wanted).astype(jnp.bfloat16)

    def adjoint_device(total, device):
        blocks = lax.dynamic_slice_in_dim(near_blocks, device * NEAR_DEV, NEAR_DEV).astype(jnp.float32)
        rows_here = lax.dynamic_slice_in_dim(near_rows, device * NEAR_DEV, NEAR_DEV)
        cols_here = lax.dynamic_slice_in_dim(near_cols, device * NEAR_DEV, NEAR_DEV)
        near_in = misfit[(device * CL_DEV + rows_here).astype(jnp.int32)].astype(jnp.float32)
        near_back = jnp.einsum("bij,bie->bje", blocks, near_in)
        total = total.at[(device * CL_DEV + cols_here).astype(jnp.int32)].add(near_back)
        left = lax.dynamic_slice_in_dim(far_left, device * FAR_DEV, FAR_DEV).astype(jnp.float32)
        right = lax.dynamic_slice_in_dim(far_right, device * FAR_DEV, FAR_DEV).astype(jnp.float32)
        frows = lax.dynamic_slice_in_dim(far_rows, device * FAR_DEV, FAR_DEV)
        fslot = lax.dynamic_slice_in_dim(far_slot, device * FAR_DEV, FAR_DEV)
        far_in = misfit[(device * CL_DEV + frows).astype(jnp.int32)].astype(jnp.float32)
        adjoint_coef = jnp.einsum("bir,bie->bre", left, far_in).astype(jnp.bfloat16)
        far_back = jnp.einsum("bir,bre->bie", right, adjoint_coef.astype(jnp.float32))
        total = total.at[far_columns(device, fslot) + 1].add(far_back)
        return total, None

    start = jnp.zeros((cluster_total + 2, LEAF, EXC), jnp.float32)
    total, unused = lax.scan(adjoint_device, start, jnp.arange(N_ROWS, dtype=jnp.int32))
    back = total[1:-1].reshape(-1, EXC)
    potentials = jnp.zeros((cluster_total * LEAF, EXC), jnp.bfloat16).at[panel_index].set(field.reshape(-1, EXC).astype(jnp.bfloat16))
    gradient = jnp.zeros((cluster_total * LEAF, EXC), jnp.float32).at[panel_index].set(back)
    return potentials, gradient
```

```python
import functools

import jax
import jax.numpy as jnp
from jax import lax
from jax.experimental import pallas as pl
from jax.experimental.pallas import tpu as pltpu
from jax.sharding import PartitionSpec as P

BF = jnp.bfloat16
F32 = jnp.float32
GROUP = 4


def dot(a, b, ca, cb):
    return lax.dot_general(a, b, (((ca,), (cb,)), ((), ())), preferred_element_type=F32)


def kernel(
    n,
    charges,
    targets,
    order,
    near_hbm,
    nrows,
    ncols,
    fleft,
    fright,
    frows,
    fslot,
    ftable,
    pot,
    grad,
    near,
    pt,
    ext,
    want,
    fr4,
    fl4,
    rslot,
    rin,
    lslot,
    cbuf,
    cin,
    abuf,
    ain,
    field,
    misfit,
    back,
    rimbuf,
    rimin,
    rowtab,
    near_sem,
    r_send,
    r_recv,
    c_send,
    c_recv,
    a_send,
    a_recv,
    e_send,
    e_recv,
    b_send,
    b_recv,
):
    me = lax.axis_index("rows")
    left, right = me - 1, me + 1
    panels, exc = charges.shape
    nears, leaf, _ = near.shape
    fars, _, rank = fleft.shape
    cap = ftable.shape[1] // n
    cl = panels // leaf
    wide = cap * rank

    near_copy = pltpu.make_async_copy(near_hbm, near, near_sem)
    near_copy.start()
    barrier = pltpu.get_barrier_semaphore()

    @pl.loop(1, n)
    def _(d):
        pl.semaphore_signal(
            barrier,
            inc=1,
            device_id={"rows": lax.rem(me + d, n)},
            device_id_type=pl.DeviceIdType.MESH,
        )

    lane_slot = lax.broadcasted_iota(jnp.int32, (1, wide), 1) // rank
    spread = (
        lax.broadcasted_iota(jnp.int32, (rank, wide), 0)
        == lax.broadcasted_iota(jnp.int32, (rank, wide), 1) % rank
    ).astype(F32).astype(BF)
    fr4[...] = dot(fright[...].reshape(fars * leaf, rank), spread, 1, 0).astype(BF).reshape(fars, leaf, wide)

    def place(table, s):
        slots = lane_slot + s * cap

        def some(g, acc):
            for k in range(16):
                b = g * 16 + k
                hot = (slots == fslot[b]).astype(F32).astype(BF)
                acc = acc + table[b] * hot
            return acc

        zero = jnp.zeros((leaf, wide), BF)
        if fars == 16:
            return some(0, zero)
        return lax.fori_loop(0, fars // 16, some, zero)

    def send(src, dst, send_sem, recv_sem, d):
        return pltpu.make_async_remote_copy(
            src_ref=src,
            dst_ref=dst,
            send_sem=send_sem,
            recv_sem=recv_sem,
            device_id={"rows": d},
            device_id_type=pl.DeviceIdType.MESH,
        )

    @pl.loop(0, n)
    def _(s):
        rslot[s] = place(fr4, s)

    rin[me] = rslot[me]
    pl.semaphore_wait(barrier, n - 1)

    @pl.loop(1, n)
    def _(d):
        t = lax.rem(me + d, n)
        send(rslot.at[t], rin.at[me], r_send.at[d], r_recv.at[d], t).start()

    pt[...] = (
        lax.broadcasted_iota(jnp.int32, (panels, panels), 0) == order[...]
    ).astype(F32).astype(BF)
    both = jnp.concatenate([charges[...], targets[...]], axis=1)
    sorted_t = dot(both, pt[...], 0, 0).astype(BF)
    for c in range(cl):
        ext[c + 1] = sorted_t[:exc, c * leaf : (c + 1) * leaf]
        want[pl.ds(c * exc, exc), :] = sorted_t[exc:, c * leaf : (c + 1) * leaf].astype(F32)

    to_left = send(ext.at[1], ext.at[cl + 1], e_send.at[0], e_recv.at[0], left)
    to_right = send(ext.at[cl], ext.at[0], e_send.at[1], e_recv.at[1], right)

    @pl.when(me > 0)
    def _():
        to_left.start()

    @pl.when(me < n - 1)
    def _():
        to_right.start()

    fl4[...] = dot(fleft[...].reshape(fars * leaf, rank), spread, 1, 0).astype(BF).reshape(fars, leaf, wide)

    @pl.loop(0, n)
    def _(s):
        lslot[s] = place(fl4, s)
        slots = lane_slot + s * cap

        def some(g, acc):
            for k in range(16):
                b = g * 16 + k
                acc = jnp.where(slots == fslot[b], frows[b], acc)
            return acc

        rowtab[pl.ds(s, 1), :] = lax.fori_loop(0, fars // 16, some, jnp.zeros((1, wide), jnp.int32))

    @pl.when(me < n - 1)
    def _():
        to_left.wait_recv()

    @pl.when(me == n - 1)
    def _():
        ext[cl + 1] = jnp.zeros((exc, leaf), BF)

    @pl.when(me > 0)
    def _():
        to_right.wait_recv()

    @pl.when(me == 0)
    def _():
        ext[0] = jnp.zeros((exc, leaf), BF)

    near_copy.wait()
    nothing = jnp.zeros((exc, leaf), BF)

    def stacked(value, place_of, count):
        return jnp.concatenate(
            [lax.select(place_of == r, value, nothing) for r in range(count)], axis=0
        )

    field[...] = jnp.zeros(field.shape, F32)

    @pl.loop(0, nears // GROUP)
    def _(g):
        ins, blocks = [], []
        for k in range(GROUP):
            b = g * GROUP + k
            ins.append(stacked(ext[ncols[b]], nrows[b], cl))
            blocks.append(near[b])
        field[...] += dot(jnp.concatenate(ins, axis=1), jnp.concatenate(blocks, axis=1), 1, 1)

    def owner_row(t):
        row = jnp.full((1, wide), -1, jnp.int32)
        for k in range(cap):
            row = jnp.where(lane_slot == k, ftable[0, t * cap + k], row)
        return row

    def chosen(product, row):
        total = jnp.zeros((exc, wide), F32)
        for c in range(cl):
            total = total + jnp.where(row == c, product[c * exc : (c + 1) * exc], 0.0)
        return total.astype(BF)

    def expanded(value, row):
        return jnp.concatenate(
            [value * (row == c).astype(F32).astype(BF) for c in range(cl)], axis=0
        )

    def coefs(t):
        return chosen(dot(ext[1 : cl + 1].reshape(cl * exc, leaf), rin[t], 1, 0), owner_row(t))

    cin[me] = coefs(me)

    @pl.loop(1, n)
    def _(d):
        t = lax.rem(me + n - d, n)
        send(rslot.at[me], rin.at[t], r_send.at[d], r_recv.at[d], t).wait_recv()
        cbuf[t] = coefs(t)
        send(cbuf.at[t], cin.at[me], c_send.at[d], c_recv.at[d], t).start()

    def far_out(s):
        field[...] += dot(expanded(cin[s], rowtab[pl.ds(s, 1), :]), lslot[s], 1, 1)

    far_out(me)

    @pl.loop(1, n)
    def _(d):
        s = lax.rem(me + d, n)
        send(cbuf.at[s], cin.at[s], c_send.at[d], c_recv.at[d], s).wait_recv()
        far_out(s)

    misfit[...] = (field[...] - want[...]).astype(BF).reshape(misfit.shape)

    def adjoint(s):
        product = dot(misfit[...].reshape(cl * exc, leaf), lslot[s], 1, 0)
        return chosen(product, rowtab[pl.ds(s, 1), :])

    @pl.loop(1, n)
    def _(d):
        s = lax.rem(me + d, n)
        abuf[s] = adjoint(s)
        send(abuf.at[s], ain.at[me], a_send.at[d], a_recv.at[d], s).start()

    ain[me] = adjoint(me)

    back[...] = jnp.zeros(back.shape, F32)

    @pl.loop(0, nears // GROUP)
    def _(g):
        ins = [
            stacked(misfit[nrows[g * GROUP + k]], ncols[g * GROUP + k], cl + 2)
            for k in range(GROUP)
        ]
        blocks = near[pl.ds(g * GROUP, GROUP)].reshape(GROUP * leaf, leaf)
        back[...] += dot(jnp.concatenate(ins, axis=1), blocks, 1, 0)

    rimbuf[0] = back[:exc].astype(BF)
    rimbuf[1] = back[(cl + 1) * exc :].astype(BF)
    rim_left = send(rimbuf.at[0], rimin.at[1], b_send.at[0], b_recv.at[0], left)
    rim_right = send(rimbuf.at[1], rimin.at[0], b_send.at[1], b_recv.at[1], right)

    @pl.when(me > 0)
    def _():
        rim_left.start()

    @pl.when(me < n - 1)
    def _():
        rim_right.start()

    inner = pl.ds(exc, cl * exc)

    def far_back(t):
        back[inner, :] += dot(expanded(ain[t], owner_row(t)), rin[t], 1, 1)

    far_back(me)

    @pl.loop(1, n)
    def _(d):
        t = lax.rem(me + n - d, n)
        send(abuf.at[t], ain.at[t], a_send.at[d], a_recv.at[d], t).wait_recv()
        far_back(t)

    @pl.when(me < n - 1)
    def _():
        rim_left.wait_recv()
        back[pl.ds(cl * exc, exc), :] += rimin[1].astype(F32)

    @pl.when(me > 0)
    def _():
        rim_right.wait_recv()
        back[pl.ds(exc, exc), :] += rimin[0].astype(F32)

    def flat(value):
        return jnp.concatenate([value[c * exc : (c + 1) * exc] for c in range(cl)], axis=1)

    full = flat(back[inner, :])
    high = full.astype(BF)
    rest = full - high.astype(F32)
    mid = rest.astype(BF)
    low = (rest - mid.astype(F32)).astype(BF)
    parts = jnp.concatenate([high, mid, flat(field[...]).astype(BF), low], axis=0)
    result = dot(pt[...], parts, 1, 1)
    pot[...] = result[:, 2 * exc : 3 * exc].astype(BF)
    grad[...] = (result[:, exc : 2 * exc] + result[:, 3 * exc :]) + result[:, :exc]

    @pl.loop(1, n)
    def _(d):
        t = lax.rem(me + d, n)
        s = lax.rem(me + n - d, n)
        send(rslot.at[t], rin.at[me], r_send.at[d], r_recv.at[d], t).wait_send()
        send(cbuf.at[s], cin.at[me], c_send.at[d], c_recv.at[d], s).wait_send()
        send(abuf.at[t], ain.at[me], a_send.at[d], a_recv.at[d], t).wait_send()

    @pl.when(me > 0)
    def _():
        to_left.wait_send()
        rim_left.wait_send()

    @pl.when(me < n - 1)
    def _():
        to_right.wait_send()
        rim_right.wait_send()


def shards(
    charges,
    targets,
    panel_order,
    near_blocks,
    near_rows,
    near_cols,
    far_left,
    far_right,
    far_rows,
    far_slot,
    far_table,
):
    n = lax.axis_size("rows")
    panels, exc = charges.shape
    nears, leaf, _ = near_blocks.shape
    fars, _, rank = far_left.shape
    cl = panels // leaf
    wide = far_table.shape[1] // n * rank
    vmem = pl.BlockSpec(memory_space=pltpu.VMEM)
    smem = pl.BlockSpec(memory_space=pltpu.SMEM)
    anywhere = pl.BlockSpec(memory_space=pl.ANY)
    sems = pltpu.SemaphoreType.DMA((n,))
    pair = pltpu.SemaphoreType.DMA((2,))
    return pl.pallas_call(
        functools.partial(kernel, n),
        out_shape=(
            jax.ShapeDtypeStruct((panels, exc), BF),
            jax.ShapeDtypeStruct((panels, exc), F32),
        ),
        in_specs=[vmem, vmem, vmem, anywhere, smem, smem, vmem, vmem, smem, smem, smem],
        out_specs=(vmem, vmem),
        scratch_shapes=[
            pltpu.VMEM((nears, leaf, leaf), BF),
            pltpu.VMEM((panels, panels), BF),
            pltpu.VMEM((cl + 2, exc, leaf), BF),
            pltpu.VMEM((cl * exc, leaf), F32),
            pltpu.VMEM((fars, leaf, wide), BF),
            pltpu.VMEM((fars, leaf, wide), BF),
            pltpu.VMEM((n, leaf, wide), BF),
            pltpu.VMEM((n, leaf, wide), BF),
            pltpu.VMEM((n, leaf, wide), BF),
            pltpu.VMEM((n, exc, wide), BF),
            pltpu.VMEM((n, exc, wide), BF),
            pltpu.VMEM((n, exc, wide), BF),
            pltpu.VMEM((n, exc, wide), BF),
            pltpu.VMEM((cl * exc, leaf), F32),
            pltpu.VMEM((cl, exc, leaf), BF),
            pltpu.VMEM(((cl + 2) * exc, leaf), F32),
            pltpu.VMEM((2, exc, leaf), BF),
            pltpu.VMEM((2, exc, leaf), BF),
            pltpu.VMEM((n, wide), jnp.int32),
            pltpu.SemaphoreType.DMA,
            sems,
            sems,
            sems,
            sems,
            sems,
            sems,
            pair,
            pair,
            pair,
            pair,
        ],
        compiler_params=pltpu.CompilerParams(
            collective_id=0, has_side_effects=True, vmem_limit_bytes=56 * 2**20
        ),
    )(
        charges,
        targets,
        panel_order,
        near_blocks,
        near_rows,
        near_cols,
        far_left,
        far_right,
        far_rows,
        far_slot,
        far_table,
    )


def solution(mesh):
    in_specs = (
        P(("groups", "rows"), None),
        P(("groups", "rows"), None),
        P(("groups", "rows"), None),
        P(("groups", "rows"), None, None),
        P(("groups", "rows")),
        P(("groups", "rows")),
        P(("groups", "rows"), None, None),
        P(("groups", "rows"), None, None),
        P(("groups", "rows")),
        P(("groups", "rows")),
        P(("groups", "rows"), None),
    )
    out_specs = (P(("groups", "rows"), None), P(("groups", "rows"), None))
    return jax.shard_map(shards, mesh=mesh, in_specs=in_specs, out_specs=out_specs, check_vma=False)
```

```python
import functools

import jax
import jax.numpy as jnp
from jax import lax
from jax.experimental import pallas as pl
from jax.experimental.pallas import tpu as pltpu
from jax.sharding import PartitionSpec as P

BF = jnp.bfloat16
F32 = jnp.float32
GROUP = 4


def dot(a, b, ca, cb):
    return lax.dot_general(a, b, (((ca,), (cb,)), ((), ())), preferred_element_type=F32)


def kernel(
    n,
    charges,
    targets,
    order,
    near_hbm,
    nrows,
    ncols,
    fleft,
    fright,
    frows,
    fslot,
    ftable,
    pot,
    grad,
    near,
    pt,
    ext,
    want,
    factors,
    target,
    rslot,
    rin,
    lslot,
    cbuf,
    cin,
    abuf,
    ain,
    field,
    misfit,
    back,
    rimbuf,
    rimin,
    rowtab,
    near_sem,
    r_send,
    r_recv,
    c_send,
    c_recv,
    a_send,
    a_recv,
    e_send,
    e_recv,
    b_send,
    b_recv,
):
    me = lax.axis_index("rows")
    left, right = me - 1, me + 1
    exc, panels = charges.shape
    nears, leaf, _ = near.shape
    fars, rank, _ = fleft.shape
    cap = ftable.shape[1] // n
    cl = panels // leaf
    wide = cap * rank

    near_copy = pltpu.make_async_copy(near_hbm, near, near_sem)
    near_copy.start()
    barrier = pltpu.get_barrier_semaphore()

    @pl.loop(1, n)
    def _(d):
        pl.semaphore_signal(
            barrier,
            inc=1,
            device_id={"rows": lax.rem(me + d, n)},
            device_id_type=pl.DeviceIdType.MESH,
        )

    lane_slot = lax.broadcasted_iota(jnp.int32, (1, wide), 1) // rank
    factors[:, :leaf] = fright[...].reshape(fars * rank, leaf)
    factors[:, leaf:] = fleft[...].reshape(fars * rank, leaf)
    for b in range(fars):
        rank_lane = lax.broadcasted_iota(jnp.int32, (1, rank), 1)
        target[:, b * rank : (b + 1) * rank] = fslot[b] * rank + rank_lane

    def send(src, dst, send_sem, recv_sem, d):
        return pltpu.make_async_remote_copy(
            src_ref=src,
            dst_ref=dst,
            send_sem=send_sem,
            recv_sem=recv_sem,
            device_id={"rows": d},
            device_id_type=pl.DeviceIdType.MESH,
        )

    @pl.loop(0, n // GROUP)
    def _(g):
        shape = (GROUP * wide, fars * rank)
        hot = lax.broadcasted_iota(jnp.int32, shape, 0) + g * (GROUP * wide) == target[...]
        placed = dot(hot.astype(F32).astype(BF), factors[...], 1, 0).astype(BF)
        rslot[pl.ds(g * GROUP, GROUP)] = placed[:, :leaf].reshape(GROUP, wide, leaf)
        lslot[pl.ds(g * GROUP, GROUP)] = placed[:, leaf:].reshape(GROUP, wide, leaf)

    rin[me] = rslot[me]
    pl.semaphore_wait(barrier, n - 1)

    @pl.loop(1, n)
    def _(d):
        t = lax.rem(me + d, n)
        send(rslot.at[t], rin.at[me], r_send.at[d], r_recv.at[d], t).start()

    pt[...] = (
        lax.broadcasted_iota(jnp.int32, (panels, panels), 0) == order[...]
    ).astype(F32).astype(BF)
    both = jnp.concatenate([charges[...], targets[...]], axis=0)
    sorted_t = dot(both, pt[...], 1, 0).astype(BF)
    for c in range(cl):
        ext[c + 1] = sorted_t[:exc, c * leaf : (c + 1) * leaf]
        want[pl.ds(c * exc, exc), :] = sorted_t[exc:, c * leaf : (c + 1) * leaf].astype(F32)

    to_left = send(ext.at[1], ext.at[cl + 1], e_send.at[0], e_recv.at[0], left)
    to_right = send(ext.at[cl], ext.at[0], e_send.at[1], e_recv.at[1], right)

    @pl.when(me > 0)
    def _():
        to_left.start()

    @pl.when(me < n - 1)
    def _():
        to_right.start()

    @pl.loop(0, n)
    def _(s):
        slots = lane_slot + s * cap

        def some(g, acc):
            for k in range(16):
                b = g * 16 + k
                acc = jnp.where(slots == fslot[b], frows[b], acc)
            return acc

        rowtab[pl.ds(s, 1), :] = lax.fori_loop(0, fars // 16, some, jnp.zeros((1, wide), jnp.int32))

    @pl.when(me < n - 1)
    def _():
        to_left.wait_recv()

    @pl.when(me == n - 1)
    def _():
        ext[cl + 1] = jnp.zeros((exc, leaf), BF)

    @pl.when(me > 0)
    def _():
        to_right.wait_recv()

    @pl.when(me == 0)
    def _():
        ext[0] = jnp.zeros((exc, leaf), BF)

    near_copy.wait()
    nothing = jnp.zeros((exc, leaf), BF)

    def stacked(value, place_of, count):
        return jnp.concatenate(
            [lax.select(place_of == r, value, nothing) for r in range(count)], axis=0
        )

    field[...] = jnp.zeros(field.shape, F32)

    @pl.loop(0, nears // GROUP)
    def _(g):
        ins, blocks = [], []
        for k in range(GROUP):
            b = g * GROUP + k
            ins.append(stacked(ext[ncols[b]], nrows[b], cl))
            blocks.append(near[b])
        field[...] += dot(jnp.concatenate(ins, axis=1), jnp.concatenate(blocks, axis=1), 1, 1)

    def owner_row(t):
        row = jnp.full((1, wide), -1, jnp.int32)
        for k in range(cap):
            row = jnp.where(lane_slot == k, ftable[0, t * cap + k], row)
        return row

    def chosen(product, row):
        total = jnp.zeros((exc, wide), F32)
        for c in range(cl):
            total = total + jnp.where(row == c, product[c * exc : (c + 1) * exc], 0.0)
        return total.astype(BF)

    def expanded(value, row):
        return jnp.concatenate(
            [value * (row == c).astype(F32).astype(BF) for c in range(cl)], axis=0
        )

    def coefs(t):
        return chosen(dot(ext[1 : cl + 1].reshape(cl * exc, leaf), rin[t], 1, 1), owner_row(t))

    cin[me] = coefs(me)

    @pl.loop(1, n)
    def _(d):
        t = lax.rem(me + n - d, n)
        send(rslot.at[me], rin.at[t], r_send.at[d], r_recv.at[d], t).wait_recv()
        cbuf[t] = coefs(t)
        send(cbuf.at[t], cin.at[me], c_send.at[d], c_recv.at[d], t).start()

    def far_out(s):
        field[...] += dot(expanded(cin[s], rowtab[pl.ds(s, 1), :]), lslot[s], 1, 0)

    far_out(me)

    @pl.loop(1, n)
    def _(d):
        s = lax.rem(me + d, n)
        send(cbuf.at[s], cin.at[s], c_send.at[d], c_recv.at[d], s).wait_recv()
        far_out(s)

    misfit[...] = (field[...] - want[...]).astype(BF).reshape(misfit.shape)

    def adjoint(s):
        product = dot(misfit[...].reshape(cl * exc, leaf), lslot[s], 1, 1)
        return chosen(product, rowtab[pl.ds(s, 1), :])

    @pl.loop(1, n)
    def _(d):
        s = lax.rem(me + d, n)
        abuf[s] = adjoint(s)
        send(abuf.at[s], ain.at[me], a_send.at[d], a_recv.at[d], s).start()

    ain[me] = adjoint(me)

    back[...] = jnp.zeros(back.shape, F32)

    @pl.loop(0, nears // GROUP)
    def _(g):
        ins = [
            stacked(misfit[nrows[g * GROUP + k]], ncols[g * GROUP + k], cl + 2)
            for k in range(GROUP)
        ]
        blocks = near[pl.ds(g * GROUP, GROUP)].reshape(GROUP * leaf, leaf)
        back[...] += dot(jnp.concatenate(ins, axis=1), blocks, 1, 0)

    rimbuf[0] = back[:exc].astype(BF)
    rimbuf[1] = back[(cl + 1) * exc :].astype(BF)
    rim_left = send(rimbuf.at[0], rimin.at[1], b_send.at[0], b_recv.at[0], left)
    rim_right = send(rimbuf.at[1], rimin.at[0], b_send.at[1], b_recv.at[1], right)

    @pl.when(me > 0)
    def _():
        rim_left.start()

    @pl.when(me < n - 1)
    def _():
        rim_right.start()

    inner = pl.ds(exc, cl * exc)

    def far_back(t):
        back[inner, :] += dot(expanded(ain[t], owner_row(t)), rin[t], 1, 0)

    far_back(me)

    @pl.loop(1, n)
    def _(d):
        t = lax.rem(me + n - d, n)
        send(abuf.at[t], ain.at[t], a_send.at[d], a_recv.at[d], t).wait_recv()
        far_back(t)

    @pl.when(me < n - 1)
    def _():
        rim_left.wait_recv()
        back[pl.ds(cl * exc, exc), :] += rimin[1].astype(F32)

    @pl.when(me > 0)
    def _():
        rim_right.wait_recv()
        back[pl.ds(exc, exc), :] += rimin[0].astype(F32)

    def flat(value):
        return jnp.concatenate([value[c * exc : (c + 1) * exc] for c in range(cl)], axis=1)

    full = flat(back[inner, :])
    high = full.astype(BF)
    rest = full - high.astype(F32)
    mid = rest.astype(BF)
    low = (rest - mid.astype(F32)).astype(BF)
    parts = jnp.concatenate([high, mid, flat(field[...]).astype(BF), low], axis=0)
    result = dot(parts, pt[...], 1, 1)
    pot[...] = result[2 * exc : 3 * exc].astype(BF)
    grad[...] = (result[exc : 2 * exc] + result[3 * exc :]) + result[:exc]

    @pl.loop(1, n)
    def _(d):
        t = lax.rem(me + d, n)
        s = lax.rem(me + n - d, n)
        send(rslot.at[t], rin.at[me], r_send.at[d], r_recv.at[d], t).wait_send()
        send(cbuf.at[s], cin.at[me], c_send.at[d], c_recv.at[d], s).wait_send()
        send(abuf.at[t], ain.at[me], a_send.at[d], a_recv.at[d], t).wait_send()

    @pl.when(me > 0)
    def _():
        to_left.wait_send()
        rim_left.wait_send()

    @pl.when(me < n - 1)
    def _():
        to_right.wait_send()
        rim_right.wait_send()


def shards(
    charges,
    targets,
    panel_order,
    near_blocks,
    near_rows,
    near_cols,
    far_left,
    far_right,
    far_rows,
    far_slot,
    far_table,
):
    n = lax.axis_size("rows")
    panels, exc = charges.shape
    nears, leaf, _ = near_blocks.shape
    fars, _, rank = far_left.shape
    cl = panels // leaf
    wide = far_table.shape[1] // n * rank
    vmem = pl.BlockSpec(memory_space=pltpu.VMEM)
    smem = pl.BlockSpec(memory_space=pltpu.SMEM)
    anywhere = pl.BlockSpec(memory_space=pl.ANY)
    sems = pltpu.SemaphoreType.DMA((n,))
    pair = pltpu.SemaphoreType.DMA((2,))
    potentials, gradient = pl.pallas_call(
        functools.partial(kernel, n),
        out_shape=(
            jax.ShapeDtypeStruct((exc, panels), BF),
            jax.ShapeDtypeStruct((exc, panels), F32),
        ),
        in_specs=[vmem, vmem, vmem, anywhere, smem, smem, vmem, vmem, smem, smem, smem],
        out_specs=(vmem, vmem),
        scratch_shapes=[
            pltpu.VMEM((nears, leaf, leaf), BF),
            pltpu.VMEM((panels, panels), BF),
            pltpu.VMEM((cl + 2, exc, leaf), BF),
            pltpu.VMEM((cl * exc, leaf), F32),
            pltpu.VMEM((fars * rank, 2 * leaf), BF),
            pltpu.VMEM((1, fars * rank), jnp.int32),
            pltpu.VMEM((n, wide, leaf), BF),
            pltpu.VMEM((n, wide, leaf), BF),
            pltpu.VMEM((n, wide, leaf), BF),
            pltpu.VMEM((n, exc, wide), BF),
            pltpu.VMEM((n, exc, wide), BF),
            pltpu.VMEM((n, exc, wide), BF),
            pltpu.VMEM((n, exc, wide), BF),
            pltpu.VMEM((cl * exc, leaf), F32),
            pltpu.VMEM((cl, exc, leaf), BF),
            pltpu.VMEM(((cl + 2) * exc, leaf), F32),
            pltpu.VMEM((2, exc, leaf), BF),
            pltpu.VMEM((2, exc, leaf), BF),
            pltpu.VMEM((n, wide), jnp.int32),
            pltpu.SemaphoreType.DMA,
            sems,
            sems,
            sems,
            sems,
            sems,
            sems,
            pair,
            pair,
            pair,
            pair,
        ],
        compiler_params=pltpu.CompilerParams(
            collective_id=0, has_side_effects=True, vmem_limit_bytes=56 * 2**20
        ),
    )(
        charges.T,
        targets.T,
        panel_order,
        near_blocks,
        near_rows,
        near_cols,
        far_left.transpose(0, 2, 1),
        far_right.transpose(0, 2, 1),
        far_rows,
        far_slot,
        far_table,
    )
    return potentials.T, gradient.T


def solution(mesh):
    in_specs = (
        P(("groups", "rows"), None),
        P(("groups", "rows"), None),
        P(("groups", "rows"), None),
        P(("groups", "rows"), None, None),
        P(("groups", "rows")),
        P(("groups", "rows")),
        P(("groups", "rows"), None, None),
        P(("groups", "rows"), None, None),
        P(("groups", "rows")),
        P(("groups", "rows")),
        P(("groups", "rows"), None),
    )
    out_specs = (P(("groups", "rows"), None), P(("groups", "rows"), None))
    return jax.shard_map(shards, mesh=mesh, in_specs=in_specs, out_specs=out_specs, check_vma=False)
```

```python
import functools

import jax
import jax.numpy as jnp
from jax import lax
from jax.experimental import pallas as pl
from jax.experimental.pallas import tpu as pltpu
from jax.sharding import PartitionSpec as P

BF = jnp.bfloat16
F32 = jnp.float32
GROUP = 4


def dot(a, b, ca, cb):
    return lax.dot_general(a, b, (((ca,), (cb,)), ((), ())), preferred_element_type=F32)


def kernel(
    n,
    charges,
    targets,
    order,
    near_hbm,
    nrows,
    ncols,
    fleft,
    fright,
    frows,
    fslot,
    ftable,
    pot,
    grad,
    near,
    pt,
    inverse,
    ext,
    want,
    factors,
    target,
    rslot,
    rin,
    lslot,
    cbuf,
    cin,
    abuf,
    ain,
    field,
    misfit,
    back,
    rimbuf,
    rimin,
    rowtab,
    near_sem,
    r_send,
    r_recv,
    c_send,
    c_recv,
    a_send,
    a_recv,
    e_send,
    e_recv,
    b_send,
    b_recv,
):
    me = lax.axis_index("rows")
    left, right = me - 1, me + 1
    exc, panels = charges.shape
    nears, leaf, _ = near.shape
    fars, rank, _ = fleft.shape
    cap = ftable.shape[1] // n
    cl = panels // leaf
    wide = cap * rank

    near_copy = pltpu.make_async_copy(near_hbm, near, near_sem)
    near_copy.start()
    barrier = pltpu.get_barrier_semaphore()

    @pl.loop(1, n)
    def _(d):
        pl.semaphore_signal(
            barrier,
            inc=1,
            device_id={"rows": lax.rem(me + d, n)},
            device_id_type=pl.DeviceIdType.MESH,
        )

    lane_slot = lax.broadcasted_iota(jnp.int32, (1, wide), 1) // rank
    factors[:, :leaf] = fright[...].reshape(fars * rank, leaf)
    factors[:, leaf:] = fleft[...].reshape(fars * rank, leaf)
    for b in range(fars):
        rank_lane = lax.broadcasted_iota(jnp.int32, (1, rank), 1)
        target[:, b * rank : (b + 1) * rank] = fslot[b] * rank + rank_lane

    def send(src, dst, send_sem, recv_sem, d):
        return pltpu.make_async_remote_copy(
            src_ref=src,
            dst_ref=dst,
            send_sem=send_sem,
            recv_sem=recv_sem,
            device_id={"rows": d},
            device_id_type=pl.DeviceIdType.MESH,
        )

    @pl.loop(0, n // GROUP)
    def _(g):
        shape = (GROUP * wide, fars * rank)
        hot = lax.broadcasted_iota(jnp.int32, shape, 0) + g * (GROUP * wide) == target[...]
        placed = dot(hot.astype(F32).astype(BF), factors[...], 1, 0).astype(BF)
        rslot[pl.ds(g * GROUP, GROUP)] = placed[:, :leaf].reshape(GROUP, wide, leaf)
        lslot[pl.ds(g * GROUP, GROUP)] = placed[:, leaf:].reshape(GROUP, wide, leaf)

    rin[me] = rslot[me]
    pl.semaphore_wait(barrier, n - 1)

    groups = n // GROUP

    def each(first, act):
        for k in range(GROUP):
            other = first + lax.rem(me + k, GROUP)

            @pl.when(other != me)
            def _():
                act(other)

    def group_at(g):
        return lax.rem(me // GROUP + g, groups) * GROUP

    def r_copy(t):
        return send(rslot.at[t], rin.at[me], r_send.at[t], r_recv.at[me], t)

    def r_arrival(t):
        return send(rslot.at[me], rin.at[t], r_send.at[t], r_recv.at[t], t)

    def c_copy(t):
        return send(cbuf.at[t], cin.at[me], c_send.at[t], c_recv.at[me], t)

    def c_arrival(t):
        return send(cbuf.at[t], cin.at[t], c_send.at[t], c_recv.at[t], t)

    def a_copy(t):
        return send(abuf.at[t], ain.at[me], a_send.at[t], a_recv.at[me], t)

    def a_arrival(t):
        return send(abuf.at[t], ain.at[t], a_send.at[t], a_recv.at[t], t)

    @pl.loop(0, groups)
    def _(g):
        each(group_at(g), lambda t: r_copy(t).start())

    pt[...] = (
        lax.broadcasted_iota(jnp.int32, (panels, panels), 0) == order[...]
    ).astype(F32).astype(BF)
    both = jnp.concatenate([charges[...], targets[...]], axis=0)
    sorted_t = dot(both, pt[...], 1, 0).astype(BF)
    for c in range(cl):
        ext[c + 1] = sorted_t[:exc, c * leaf : (c + 1) * leaf]
        want[pl.ds(c * exc, exc), :] = sorted_t[exc:, c * leaf : (c + 1) * leaf].astype(F32)

    to_left = send(ext.at[1], ext.at[cl + 1], e_send.at[0], e_recv.at[0], left)
    to_right = send(ext.at[cl], ext.at[0], e_send.at[1], e_recv.at[1], right)

    @pl.when(me > 0)
    def _():
        to_left.start()

    @pl.when(me < n - 1)
    def _():
        to_right.start()

    @pl.loop(0, n)
    def _(s):
        slots = lane_slot + s * cap

        def some(g, acc):
            for k in range(16):
                b = g * 16 + k
                acc = jnp.where(slots == fslot[b], frows[b], acc)
            return acc

        rowtab[s // GROUP, pl.ds(lax.rem(s, GROUP), 1)] = lax.fori_loop(0, fars // 16, some, jnp.zeros((1, wide), jnp.int32))

    @pl.when(me < n - 1)
    def _():
        to_left.wait_recv()

    @pl.when(me == n - 1)
    def _():
        ext[cl + 1] = jnp.zeros((exc, leaf), BF)

    @pl.when(me > 0)
    def _():
        to_right.wait_recv()

    @pl.when(me == 0)
    def _():
        ext[0] = jnp.zeros((exc, leaf), BF)

    near_copy.wait()
    nothing = jnp.zeros((exc, leaf), BF)

    def stacked(value, place_of, count):
        return jnp.concatenate(
            [lax.select(place_of == r, value, nothing) for r in range(count)], axis=0
        )

    field[...] = jnp.zeros(field.shape, F32)

    @pl.loop(0, nears // GROUP)
    def _(g):
        ins, blocks = [], []
        for k in range(GROUP):
            b = g * GROUP + k
            ins.append(stacked(ext[ncols[b]], nrows[b], cl))
            blocks.append(near[b])
        field[...] += dot(jnp.concatenate(ins, axis=1), jnp.concatenate(blocks, axis=1), 1, 1)

    def owner_row(first):
        rows = []
        for t in range(GROUP):
            row = jnp.full((1, wide), -1, jnp.int32)
            for k in range(cap):
                row = jnp.where(lane_slot == k, ftable[0, (first + t) * cap + k], row)
            rows.append(row)
        return jnp.concatenate(rows, axis=1)

    def target_row(first):
        return jnp.concatenate([rowtab[first // GROUP, t : t + 1] for t in range(GROUP)], axis=1)

    def chosen(value, factor, row, out, first):
        product = dot(value, factor[pl.ds(first, GROUP)].reshape(GROUP * wide, leaf), 1, 1)
        total = jnp.zeros((exc, GROUP * wide), F32)
        for c in range(cl):
            total = total + jnp.where(row == c, product[c * exc : (c + 1) * exc], 0.0)
        total = total.astype(BF)
        for t in range(GROUP):
            out[first + t] = total[:, t * wide : (t + 1) * wide]

    def expanded(value, row, factor, first):
        parts = jnp.concatenate([value[first + t] for t in range(GROUP)], axis=1)
        masks = [(row == c).astype(F32).astype(BF) for c in range(cl)]
        spread = jnp.concatenate([parts * mask for mask in masks], axis=0)
        return dot(spread, factor[pl.ds(first, GROUP)].reshape(GROUP * wide, leaf), 1, 0)

    mine = ext[1 : cl + 1].reshape(cl * exc, leaf)

    @pl.loop(0, groups)
    def _(g):
        first = group_at(groups - g)
        each(first, lambda t: r_arrival(t).wait_recv())
        chosen(mine, rin, owner_row(first), cbuf, first)
        each(first, lambda t: c_copy(t).start())

    cin[me] = cbuf[me]

    order_rows = jnp.broadcast_to(order[...].astype(F32), (8, panels))
    spot = jnp.transpose(order_rows)[:, :1]
    lanes = lax.broadcasted_iota(jnp.int32, (panels, panels), 1).astype(F32)
    inverse[...] = (lanes == spot).astype(F32).astype(BF)

    @pl.loop(0, groups)
    def _(g):
        first = group_at(g)
        each(first, lambda t: c_arrival(t).wait_recv())
        field[...] += expanded(cin, target_row(first), lslot, first)

    misfit[...] = (field[...] - want[...]).astype(BF).reshape(misfit.shape)

    @pl.loop(0, groups)
    def _(g):
        first = group_at(g)
        chosen(misfit[...].reshape(cl * exc, leaf), lslot, target_row(first), abuf, first)
        each(first, lambda t: a_copy(t).start())

    ain[me] = abuf[me]

    back[...] = jnp.zeros(back.shape, F32)

    @pl.loop(0, nears // GROUP)
    def _(g):
        ins = [
            stacked(misfit[nrows[g * GROUP + k]], ncols[g * GROUP + k], cl + 2)
            for k in range(GROUP)
        ]
        blocks = near[pl.ds(g * GROUP, GROUP)].reshape(GROUP * leaf, leaf)
        back[...] += dot(jnp.concatenate(ins, axis=1), blocks, 1, 0)

    rimbuf[0] = back[:exc].astype(BF)
    rimbuf[1] = back[(cl + 1) * exc :].astype(BF)
    rim_left = send(rimbuf.at[0], rimin.at[1], b_send.at[0], b_recv.at[0], left)
    rim_right = send(rimbuf.at[1], rimin.at[0], b_send.at[1], b_recv.at[1], right)

    @pl.when(me > 0)
    def _():
        rim_left.start()

    @pl.when(me < n - 1)
    def _():
        rim_right.start()

    inner = pl.ds(exc, cl * exc)

    @pl.loop(0, groups)
    def _(g):
        first = group_at(groups - g)
        each(first, lambda t: a_arrival(t).wait_recv())
        back[inner, :] += expanded(ain, owner_row(first), rin, first)

    @pl.when(me < n - 1)
    def _():
        rim_left.wait_recv()
        back[pl.ds(cl * exc, exc), :] += rimin[1].astype(F32)

    @pl.when(me > 0)
    def _():
        rim_right.wait_recv()
        back[pl.ds(exc, exc), :] += rimin[0].astype(F32)

    def flat(value):
        return jnp.concatenate([value[c * exc : (c + 1) * exc] for c in range(cl)], axis=1)

    full = flat(back[inner, :])
    high = full.astype(BF)
    rest = full - high.astype(F32)
    mid = rest.astype(BF)
    low = (rest - mid.astype(F32)).astype(BF)
    parts = jnp.concatenate([high, mid, flat(field[...]).astype(BF), low], axis=0)
    result = dot(parts, inverse[...], 1, 0)
    pot[...] = result[2 * exc : 3 * exc].astype(BF)
    grad[...] = (result[exc : 2 * exc] + result[3 * exc :]) + result[:exc]

    @pl.loop(0, groups)
    def _(g):
        first = group_at(g)
        each(first, lambda t: r_copy(t).wait_send())
        each(first, lambda t: c_copy(t).wait_send())
        each(first, lambda t: a_copy(t).wait_send())

    @pl.when(me > 0)
    def _():
        to_left.wait_send()
        rim_left.wait_send()

    @pl.when(me < n - 1)
    def _():
        to_right.wait_send()
        rim_right.wait_send()


def shards(
    charges,
    targets,
    panel_order,
    near_blocks,
    near_rows,
    near_cols,
    far_left,
    far_right,
    far_rows,
    far_slot,
    far_table,
):
    n = lax.axis_size("rows")
    panels, exc = charges.shape
    nears, leaf, _ = near_blocks.shape
    fars, _, rank = far_left.shape
    cl = panels // leaf
    wide = far_table.shape[1] // n * rank
    vmem = pl.BlockSpec(memory_space=pltpu.VMEM)
    smem = pl.BlockSpec(memory_space=pltpu.SMEM)
    anywhere = pl.BlockSpec(memory_space=pl.ANY)
    sems = pltpu.SemaphoreType.DMA((n,))
    pair = pltpu.SemaphoreType.DMA((2,))
    potentials, gradient = pl.pallas_call(
        functools.partial(kernel, n),
        out_shape=(
            jax.ShapeDtypeStruct((exc, panels), BF),
            jax.ShapeDtypeStruct((exc, panels), F32),
        ),
        in_specs=[vmem, vmem, vmem, anywhere, smem, smem, vmem, vmem, smem, smem, smem],
        out_specs=(vmem, vmem),
        scratch_shapes=[
            pltpu.VMEM((nears, leaf, leaf), BF),
            pltpu.VMEM((panels, panels), BF),
            pltpu.VMEM((panels, panels), BF),
            pltpu.VMEM((cl + 2, exc, leaf), BF),
            pltpu.VMEM((cl * exc, leaf), F32),
            pltpu.VMEM((fars * rank, 2 * leaf), BF),
            pltpu.VMEM((1, fars * rank), jnp.int32),
            pltpu.VMEM((n, wide, leaf), BF),
            pltpu.VMEM((n, wide, leaf), BF),
            pltpu.VMEM((n, wide, leaf), BF),
            pltpu.VMEM((n, exc, wide), BF),
            pltpu.VMEM((n, exc, wide), BF),
            pltpu.VMEM((n, exc, wide), BF),
            pltpu.VMEM((n, exc, wide), BF),
            pltpu.VMEM((cl * exc, leaf), F32),
            pltpu.VMEM((cl, exc, leaf), BF),
            pltpu.VMEM(((cl + 2) * exc, leaf), F32),
            pltpu.VMEM((2, exc, leaf), BF),
            pltpu.VMEM((2, exc, leaf), BF),
            pltpu.VMEM((n // GROUP, GROUP, wide), jnp.int32),
            pltpu.SemaphoreType.DMA,
            sems,
            sems,
            sems,
            sems,
            sems,
            sems,
            pair,
            pair,
            pair,
            pair,
        ],
        compiler_params=pltpu.CompilerParams(
            collective_id=0, has_side_effects=True, vmem_limit_bytes=56 * 2**20
        ),
    )(
        charges.T,
        targets.T,
        panel_order,
        near_blocks,
        near_rows,
        near_cols,
        far_left.transpose(0, 2, 1),
        far_right.transpose(0, 2, 1),
        far_rows,
        far_slot,
        far_table,
    )
    return potentials.T, gradient.T


def solution(mesh):
    in_specs = (
        P(("groups", "rows"), None),
        P(("groups", "rows"), None),
        P(("groups", "rows"), None),
        P(("groups", "rows"), None, None),
        P(("groups", "rows")),
        P(("groups", "rows")),
        P(("groups", "rows"), None, None),
        P(("groups", "rows"), None, None),
        P(("groups", "rows")),
        P(("groups", "rows")),
        P(("groups", "rows"), None),
    )
    out_specs = (P(("groups", "rows"), None), P(("groups", "rows"), None))
    return jax.shard_map(shards, mesh=mesh, in_specs=in_specs, out_specs=out_specs, check_vma=False)
```

```python
import functools

import jax
import jax.numpy as jnp
from jax import lax
from jax.experimental import pallas as pl
from jax.experimental.pallas import tpu as pltpu
from jax.sharding import PartitionSpec as P

BF = jnp.bfloat16
F32 = jnp.float32
GROUP = 4


def dot(a, b, ca, cb):
    return lax.dot_general(a, b, (((ca,), (cb,)), ((), ())), preferred_element_type=F32)


def kernel(
    n,
    charges,
    targets,
    order,
    near_hbm,
    nrows,
    ncols,
    fleft,
    fright,
    frows,
    fslot,
    ftable,
    parts,
    near,
    pt,
    ext,
    want,
    factors,
    target,
    rslot,
    rin,
    lslot,
    cbuf,
    cin,
    abuf,
    ain,
    field,
    misfit,
    back,
    rim,
    rimbuf,
    rimin,
    rowtab,
    near_sem,
    r_send,
    r_recv,
    c_send,
    c_recv,
    a_send,
    a_recv,
    e_send,
    e_recv,
    b_send,
    b_recv,
):
    me = lax.axis_index("rows")
    left, right = me - 1, me + 1
    exc, panels = charges.shape
    nears, leaf, _ = near.shape
    fars, rank, _ = fleft.shape
    cap = ftable.shape[1] // n
    cl = panels // leaf
    wide = cap * rank

    near_copy = pltpu.make_async_copy(near_hbm, near, near_sem)
    near_copy.start()
    barrier = pltpu.get_barrier_semaphore()

    @pl.loop(1, n)
    def _(d):
        pl.semaphore_signal(
            barrier,
            inc=1,
            device_id={"rows": lax.rem(me + d, n)},
            device_id_type=pl.DeviceIdType.MESH,
        )

    lane_slot = lax.broadcasted_iota(jnp.int32, (1, wide), 1) // rank
    factors[:, :leaf] = fright[...].reshape(fars * rank, leaf)
    factors[:, leaf:] = fleft[...].reshape(fars * rank, leaf)
    for b in range(fars):
        rank_lane = lax.broadcasted_iota(jnp.int32, (1, rank), 1)
        target[:, b * rank : (b + 1) * rank] = fslot[b] * rank + rank_lane

    def send(src, dst, send_sem, recv_sem, d):
        return pltpu.make_async_remote_copy(
            src_ref=src,
            dst_ref=dst,
            send_sem=send_sem,
            recv_sem=recv_sem,
            device_id={"rows": d},
            device_id_type=pl.DeviceIdType.MESH,
        )

    @pl.loop(0, n // GROUP)
    def _(g):
        shape = (GROUP * wide, fars * rank)
        hot = lax.broadcasted_iota(jnp.int32, shape, 0) + g * (GROUP * wide) == target[...]
        placed = dot(hot.astype(F32).astype(BF), factors[...], 1, 0).astype(BF)
        rslot[pl.ds(g * GROUP, GROUP)] = placed[:, :leaf].reshape(GROUP, wide, leaf)
        lslot[pl.ds(g * GROUP, GROUP)] = placed[:, leaf:].reshape(GROUP, wide, leaf)

    rin[me] = rslot[me]
    pl.semaphore_wait(barrier, n - 1)

    groups = n // GROUP

    def each(first, act):
        for k in range(GROUP):
            other = first + lax.rem(me + k, GROUP)

            @pl.when(other != me)
            def _():
                act(other)

    def group_at(g):
        return lax.rem(me // GROUP + g, groups) * GROUP

    def r_copy(t):
        return send(rslot.at[t], rin.at[me], r_send.at[t], r_recv.at[me], t)

    def r_arrival(t):
        return send(rslot.at[me], rin.at[t], r_send.at[t], r_recv.at[t], t)

    def c_copy(t):
        return send(cbuf.at[t], cin.at[me], c_send.at[t], c_recv.at[me], t)

    def c_arrival(t):
        return send(cbuf.at[t], cin.at[t], c_send.at[t], c_recv.at[t], t)

    def a_copy(t):
        return send(abuf.at[t], ain.at[me], a_send.at[t], a_recv.at[me], t)

    def a_arrival(t):
        return send(abuf.at[t], ain.at[t], a_send.at[t], a_recv.at[t], t)

    @pl.loop(0, groups)
    def _(g):
        each(group_at(g), lambda t: r_copy(t).start())

    pt[...] = (
        lax.broadcasted_iota(jnp.int32, (panels, panels), 0) == order[...]
    ).astype(F32).astype(BF)
    both = jnp.concatenate([charges[...], targets[...]], axis=0)
    sorted_t = dot(both, pt[...], 1, 0).astype(BF)
    for c in range(cl):
        ext[c + 1] = sorted_t[:exc, c * leaf : (c + 1) * leaf]
        want[pl.ds(c * exc, exc), :] = sorted_t[exc:, c * leaf : (c + 1) * leaf].astype(F32)

    to_left = send(ext.at[1], ext.at[cl + 1], e_send.at[0], e_recv.at[0], left)
    to_right = send(ext.at[cl], ext.at[0], e_send.at[1], e_recv.at[1], right)

    @pl.when(me > 0)
    def _():
        to_left.start()

    @pl.when(me < n - 1)
    def _():
        to_right.start()

    @pl.loop(0, n)
    def _(s):
        slots = lane_slot + s * cap

        def some(g, acc):
            for k in range(16):
                b = g * 16 + k
                acc = jnp.where(slots == fslot[b], frows[b], acc)
            return acc

        rowtab[s // GROUP, pl.ds(lax.rem(s, GROUP), 1)] = lax.fori_loop(0, fars // 16, some, jnp.zeros((1, wide), jnp.int32))

    @pl.when(me < n - 1)
    def _():
        to_left.wait_recv()

    @pl.when(me == n - 1)
    def _():
        ext[cl + 1] = jnp.zeros((exc, leaf), BF)

    @pl.when(me > 0)
    def _():
        to_right.wait_recv()

    @pl.when(me == 0)
    def _():
        ext[0] = jnp.zeros((exc, leaf), BF)

    near_copy.wait()
    nothing = jnp.zeros((exc, leaf), BF)

    def stacked(value, place_of, count):
        return jnp.concatenate(
            [lax.select(place_of == r, value, nothing) for r in range(count)], axis=0
        )

    field[...] = jnp.zeros(field.shape, F32)

    @pl.loop(0, nears // GROUP)
    def _(g):
        ins, blocks = [], []
        for k in range(GROUP):
            b = g * GROUP + k
            ins.append(stacked(ext[ncols[b]], nrows[b], cl))
            blocks.append(near[b])
        field[...] += dot(jnp.concatenate(ins, axis=1), jnp.concatenate(blocks, axis=1), 1, 1)

    def owner_row(first):
        rows = []
        for t in range(GROUP):
            row = jnp.full((1, wide), -1, jnp.int32)
            for k in range(cap):
                row = jnp.where(lane_slot == k, ftable[0, (first + t) * cap + k], row)
            rows.append(row)
        return jnp.concatenate(rows, axis=1)

    def target_row(first):
        return jnp.concatenate([rowtab[first // GROUP, t : t + 1] for t in range(GROUP)], axis=1)

    def chosen(value, factor, row, out, first):
        product = dot(value, factor[pl.ds(first, GROUP)].reshape(GROUP * wide, leaf), 1, 1)
        total = jnp.zeros((exc, GROUP * wide), F32)
        for c in range(cl):
            total = total + jnp.where(row == c, product[c * exc : (c + 1) * exc], 0.0)
        total = total.astype(BF)
        for t in range(GROUP):
            out[first + t] = total[:, t * wide : (t + 1) * wide]

    def expanded(value, row, factor, first):
        parts = jnp.concatenate([value[first + t] for t in range(GROUP)], axis=1)
        masks = [(row == c).astype(F32).astype(BF) for c in range(cl)]
        spread = jnp.concatenate([parts * mask for mask in masks], axis=0)
        return dot(spread, factor[pl.ds(first, GROUP)].reshape(GROUP * wide, leaf), 1, 0)

    mine = ext[1 : cl + 1].reshape(cl * exc, leaf)

    @pl.loop(0, groups)
    def _(g):
        first = group_at(groups - g)
        each(first, lambda t: r_arrival(t).wait_recv())
        chosen(mine, rin, owner_row(first), cbuf, first)
        each(first, lambda t: c_copy(t).start())

    cin[me] = cbuf[me]

    @pl.loop(0, groups)
    def _(g):
        first = group_at(g)
        each(first, lambda t: c_arrival(t).wait_recv())
        field[...] += expanded(cin, target_row(first), lslot, first)

    misfit[...] = (field[...] - want[...]).astype(BF).reshape(misfit.shape)

    @pl.loop(0, groups)
    def _(g):
        first = group_at(g)
        chosen(misfit[...].reshape(cl * exc, leaf), lslot, target_row(first), abuf, first)
        each(first, lambda t: a_copy(t).start())

    ain[me] = abuf[me]

    rim[...] = jnp.zeros(rim.shape, F32)

    def near_back(g, columns):
        ins = []
        for k in range(GROUP):
            b = g * GROUP + k
            value, col = misfit[nrows[b]], ncols[b]
            ins.append(
                jnp.concatenate([lax.select(col == c, value, nothing) for c in columns], axis=0)
            )
        blocks = near[pl.ds(g * GROUP, GROUP)].reshape(GROUP * leaf, leaf)
        return dot(jnp.concatenate(ins, axis=1), blocks, 1, 0)

    @pl.loop(0, nears // GROUP)
    def _(g):
        rim[...] += near_back(g, (0, cl + 1))

    rimbuf[0] = rim[:exc].astype(BF)
    rimbuf[1] = rim[exc:].astype(BF)
    rim_left = send(rimbuf.at[0], rimin.at[1], b_send.at[0], b_recv.at[0], left)
    rim_right = send(rimbuf.at[1], rimin.at[0], b_send.at[1], b_recv.at[1], right)

    @pl.when(me > 0)
    def _():
        rim_left.start()

    @pl.when(me < n - 1)
    def _():
        rim_right.start()

    back[...] = jnp.zeros(back.shape, F32)

    @pl.loop(0, nears // GROUP)
    def _(g):
        back[...] += near_back(g, range(1, cl + 1))


    @pl.loop(0, groups)
    def _(g):
        first = group_at(groups - g)
        each(first, lambda t: a_arrival(t).wait_recv())
        back[...] += expanded(ain, owner_row(first), rin, first)

    @pl.when(me < n - 1)
    def _():
        rim_left.wait_recv()
        back[pl.ds((cl - 1) * exc, exc), :] += rimin[1].astype(F32)

    @pl.when(me > 0)
    def _():
        rim_right.wait_recv()
        back[pl.ds(0, exc), :] += rimin[0].astype(F32)

    def flat(value):
        return jnp.concatenate([value[c * exc : (c + 1) * exc] for c in range(cl)], axis=1)

    full = flat(back[...])
    high = full.astype(BF)
    rest = full - high.astype(F32)
    mid = rest.astype(BF)
    low = (rest - mid.astype(F32)).astype(BF)
    parts[...] = jnp.concatenate([high, mid, flat(field[...]).astype(BF), low], axis=0)

    @pl.loop(0, groups)
    def _(g):
        first = group_at(g)
        each(first, lambda t: r_copy(t).wait_send())
        each(first, lambda t: c_copy(t).wait_send())
        each(first, lambda t: a_copy(t).wait_send())

    @pl.when(me > 0)
    def _():
        to_left.wait_send()
        rim_left.wait_send()

    @pl.when(me < n - 1)
    def _():
        to_right.wait_send()
        rim_right.wait_send()


def unsort(order, parts, pot, grad):
    exc, panels = pot.shape
    spot = jnp.transpose(jnp.broadcast_to(order[...].astype(F32), (8, panels)))[:, :1]
    lanes = lax.broadcasted_iota(jnp.int32, (panels, panels), 1).astype(F32)
    inverse = (lanes == spot).astype(F32).astype(BF)
    result = dot(parts[...], inverse, 1, 0)
    pot[...] = result[2 * exc : 3 * exc].astype(BF)
    grad[...] = (result[exc : 2 * exc] + result[3 * exc :]) + result[:exc]


def shards(
    charges,
    targets,
    panel_order,
    near_blocks,
    near_rows,
    near_cols,
    far_left,
    far_right,
    far_rows,
    far_slot,
    far_table,
):
    n = lax.axis_size("rows")
    panels, exc = charges.shape
    nears, leaf, _ = near_blocks.shape
    fars, _, rank = far_left.shape
    cl = panels // leaf
    wide = far_table.shape[1] // n * rank
    vmem = pl.BlockSpec(memory_space=pltpu.VMEM)
    smem = pl.BlockSpec(memory_space=pltpu.SMEM)
    anywhere = pl.BlockSpec(memory_space=pl.ANY)
    sems = pltpu.SemaphoreType.DMA((n,))
    pair = pltpu.SemaphoreType.DMA((2,))
    parts = pl.pallas_call(
        functools.partial(kernel, n),
        out_shape=jax.ShapeDtypeStruct((4 * exc, panels), BF),
        in_specs=[vmem, vmem, vmem, anywhere, smem, smem, vmem, vmem, smem, smem, smem],
        out_specs=vmem,
        scratch_shapes=[
            pltpu.VMEM((nears, leaf, leaf), BF),
            pltpu.VMEM((panels, panels), BF),
            pltpu.VMEM((cl + 2, exc, leaf), BF),
            pltpu.VMEM((cl * exc, leaf), F32),
            pltpu.VMEM((fars * rank, 2 * leaf), BF),
            pltpu.VMEM((1, fars * rank), jnp.int32),
            pltpu.VMEM((n, wide, leaf), BF),
            pltpu.VMEM((n, wide, leaf), BF),
            pltpu.VMEM((n, wide, leaf), BF),
            pltpu.VMEM((n, exc, wide), BF),
            pltpu.VMEM((n, exc, wide), BF),
            pltpu.VMEM((n, exc, wide), BF),
            pltpu.VMEM((n, exc, wide), BF),
            pltpu.VMEM((cl * exc, leaf), F32),
            pltpu.VMEM((cl, exc, leaf), BF),
            pltpu.VMEM((cl * exc, leaf), F32),
            pltpu.VMEM((2 * exc, leaf), F32),
            pltpu.VMEM((2, exc, leaf), BF),
            pltpu.VMEM((2, exc, leaf), BF),
            pltpu.VMEM((n // GROUP, GROUP, wide), jnp.int32),
            pltpu.SemaphoreType.DMA,
            sems,
            sems,
            sems,
            sems,
            sems,
            sems,
            pair,
            pair,
            pair,
            pair,
        ],
        compiler_params=pltpu.CompilerParams(
            collective_id=0, has_side_effects=True, vmem_limit_bytes=56 * 2**20
        ),
    )(
        charges.T,
        targets.T,
        panel_order,
        near_blocks,
        near_rows,
        near_cols,
        far_left.transpose(0, 2, 1),
        far_right.transpose(0, 2, 1),
        far_rows,
        far_slot,
        far_table,
    )
    potentials, gradient = pl.pallas_call(
        unsort,
        out_shape=(
            jax.ShapeDtypeStruct((exc, panels), BF),
            jax.ShapeDtypeStruct((exc, panels), F32),
        ),
        in_specs=[vmem, vmem],
        out_specs=(vmem, vmem),
        compiler_params=pltpu.CompilerParams(vmem_limit_bytes=32 * 2**20),
    )(panel_order, parts)
    return potentials.T, gradient.T


def solution(mesh):
    in_specs = (
        P(("groups", "rows"), None),
        P(("groups", "rows"), None),
        P(("groups", "rows"), None),
        P(("groups", "rows"), None, None),
        P(("groups", "rows")),
        P(("groups", "rows")),
        P(("groups", "rows"), None, None),
        P(("groups", "rows"), None, None),
        P(("groups", "rows")),
        P(("groups", "rows")),
        P(("groups", "rows"), None),
    )
    out_specs = (P(("groups", "rows"), None), P(("groups", "rows"), None))
    return jax.shard_map(shards, mesh=mesh, in_specs=in_specs, out_specs=out_specs, check_vma=False)
```

```python
import functools

import jax
import jax.numpy as jnp
from jax import lax
from jax.experimental import pallas as pl
from jax.experimental.pallas import tpu as pltpu
from jax.sharding import PartitionSpec as P

BF = jnp.bfloat16
F32 = jnp.float32
GROUP = 4
NEAR_GROUP = 16


def dot(a, b, ca, cb):
    return lax.dot_general(a, b, (((ca,), (cb,)), ((), ())), preferred_element_type=F32)


def kernel(
    n,
    charges,
    targets,
    order,
    near_hbm,
    nrows,
    ncols,
    fleft,
    fright,
    frows,
    fslot,
    ftable,
    parts,
    near,
    pt,
    ext,
    want,
    factors,
    target,
    rslot,
    rin,
    lslot,
    cbuf,
    cin,
    abuf,
    ain,
    field,
    misfit,
    back,
    rimbuf,
    rimin,
    rowtab,
    near_sem,
    r_send,
    r_recv,
    c_send,
    c_recv,
    a_send,
    a_recv,
    e_send,
    e_recv,
    b_send,
    b_recv,
):
    me = lax.axis_index("rows")
    left, right = me - 1, me + 1
    exc, panels = charges.shape
    nears, leaf, _ = near.shape
    fars, rank, _ = fleft.shape
    cap = ftable.shape[1] // n
    cl = panels // leaf
    wide = cap * rank

    near_copy = pltpu.make_async_copy(near_hbm, near, near_sem)
    near_copy.start()
    barrier = pltpu.get_barrier_semaphore()

    @pl.loop(1, n)
    def _(d):
        pl.semaphore_signal(
            barrier,
            inc=1,
            device_id={"rows": lax.rem(me + d, n)},
            device_id_type=pl.DeviceIdType.MESH,
        )

    lane_slot = lax.broadcasted_iota(jnp.int32, (1, wide), 1) // rank
    factors[:, :leaf] = fright[...].reshape(fars * rank, leaf)
    factors[:, leaf:] = fleft[...].reshape(fars * rank, leaf)
    for b in range(fars):
        rank_lane = lax.broadcasted_iota(jnp.int32, (1, rank), 1)
        target[:, b * rank : (b + 1) * rank] = fslot[b] * rank + rank_lane

    def send(src, dst, send_sem, recv_sem, d):
        return pltpu.make_async_remote_copy(
            src_ref=src,
            dst_ref=dst,
            send_sem=send_sem,
            recv_sem=recv_sem,
            device_id={"rows": d},
            device_id_type=pl.DeviceIdType.MESH,
        )

    @pl.loop(0, n // GROUP)
    def _(g):
        shape = (GROUP * wide, fars * rank)
        hot = lax.broadcasted_iota(jnp.int32, shape, 0) + g * (GROUP * wide) == target[...]
        placed = dot(hot.astype(F32).astype(BF), factors[...], 1, 0).astype(BF)
        rslot[pl.ds(g * GROUP, GROUP)] = placed[:, :leaf].reshape(GROUP, wide, leaf)
        lslot[pl.ds(g * GROUP, GROUP)] = placed[:, leaf:].reshape(GROUP, wide, leaf)

    rin[me] = rslot[me]
    pl.semaphore_wait(barrier, n - 1)

    groups = n // GROUP

    def each(first, act):
        for k in range(GROUP):
            other = first + lax.rem(me + k, GROUP)

            @pl.when(other != me)
            def _():
                act(other)

    def group_at(g):
        return lax.rem(me // GROUP + g, groups) * GROUP

    def r_copy(t):
        return send(rslot.at[t], rin.at[me], r_send.at[t], r_recv.at[me], t)

    def r_arrival(t):
        return send(rslot.at[me], rin.at[t], r_send.at[t], r_recv.at[t], t)

    def c_copy(t):
        return send(cbuf.at[t], cin.at[me], c_send.at[t], c_recv.at[me], t)

    def c_arrival(t):
        return send(cbuf.at[t], cin.at[t], c_send.at[t], c_recv.at[t], t)

    def a_copy(t):
        return send(abuf.at[t], ain.at[me], a_send.at[t], a_recv.at[me], t)

    def a_arrival(t):
        return send(abuf.at[t], ain.at[t], a_send.at[t], a_recv.at[t], t)

    @pl.loop(0, groups)
    def _(g):
        each(group_at(g), lambda t: r_copy(t).start())

    pt[...] = (
        lax.broadcasted_iota(jnp.int32, (panels, panels), 0) == order[...]
    ).astype(F32).astype(BF)
    both = jnp.concatenate([charges[...], targets[...]], axis=0)
    sorted_t = dot(both, pt[...], 1, 0).astype(BF)
    for c in range(cl):
        ext[c + 1] = sorted_t[:exc, c * leaf : (c + 1) * leaf]
        want[pl.ds(c * exc, exc), :] = sorted_t[exc:, c * leaf : (c + 1) * leaf].astype(F32)

    to_left = send(ext.at[1], ext.at[cl + 1], e_send.at[0], e_recv.at[0], left)
    to_right = send(ext.at[cl], ext.at[0], e_send.at[1], e_recv.at[1], right)

    @pl.when(me > 0)
    def _():
        to_left.start()

    @pl.when(me < n - 1)
    def _():
        to_right.start()

    @pl.loop(0, n)
    def _(s):
        slots = lane_slot + s * cap

        def some(g, acc):
            for k in range(16):
                b = g * 16 + k
                acc = jnp.where(slots == fslot[b], frows[b], acc)
            return acc

        rowtab[s // GROUP, pl.ds(lax.rem(s, GROUP), 1)] = lax.fori_loop(0, fars // 16, some, jnp.zeros((1, wide), jnp.int32))

    @pl.when(me < n - 1)
    def _():
        to_left.wait_recv()

    @pl.when(me == n - 1)
    def _():
        ext[cl + 1] = jnp.zeros((exc, leaf), BF)

    @pl.when(me > 0)
    def _():
        to_right.wait_recv()

    @pl.when(me == 0)
    def _():
        ext[0] = jnp.zeros((exc, leaf), BF)

    near_copy.wait()
    nothing = jnp.zeros((exc, leaf), BF)

    def stacked(value, place_of, count):
        return jnp.concatenate(
            [lax.select(place_of == r, value, nothing) for r in range(count)], axis=0
        )

    field[...] = jnp.zeros(field.shape, F32)

    @pl.loop(0, nears // NEAR_GROUP)
    def _(g):
        ins, blocks = [], []
        for k in range(NEAR_GROUP):
            b = g * NEAR_GROUP + k
            ins.append(stacked(ext[ncols[b]], nrows[b], cl))
            blocks.append(near[b])
        field[...] += dot(jnp.concatenate(ins, axis=1), jnp.concatenate(blocks, axis=1), 1, 1)

    def owner_row(first):
        rows = []
        for t in range(GROUP):
            row = jnp.full((1, wide), -1, jnp.int32)
            for k in range(cap):
                row = jnp.where(lane_slot == k, ftable[0, (first + t) * cap + k], row)
            rows.append(row)
        return jnp.concatenate(rows, axis=1)

    def target_row(first):
        return jnp.concatenate([rowtab[first // GROUP, t : t + 1] for t in range(GROUP)], axis=1)

    def chosen(value, factor, row, out, first):
        product = dot(value, factor[pl.ds(first, GROUP)].reshape(GROUP * wide, leaf), 1, 1)
        total = jnp.zeros((exc, GROUP * wide), F32)
        for c in range(cl):
            total = total + jnp.where(row == c, product[c * exc : (c + 1) * exc], 0.0)
        total = total.astype(BF)
        for t in range(GROUP):
            out[first + t] = total[:, t * wide : (t + 1) * wide]

    def expanded(value, row, factor, first):
        parts = jnp.concatenate([value[first + t] for t in range(GROUP)], axis=1)
        masks = [(row == c).astype(F32).astype(BF) for c in range(cl)]
        spread = jnp.concatenate([parts * mask for mask in masks], axis=0)
        return dot(spread, factor[pl.ds(first, GROUP)].reshape(GROUP * wide, leaf), 1, 0)

    mine = ext[1 : cl + 1].reshape(cl * exc, leaf)

    @pl.loop(0, groups)
    def _(g):
        first = group_at(groups - g)
        each(first, lambda t: r_arrival(t).wait_recv())
        chosen(mine, rin, owner_row(first), cbuf, first)
        each(first, lambda t: c_copy(t).start())

    cin[me] = cbuf[me]

    @pl.loop(0, groups)
    def _(g):
        first = group_at(g)
        each(first, lambda t: c_arrival(t).wait_recv())
        field[...] += expanded(cin, target_row(first), lslot, first)

    misfit[...] = (field[...] - want[...]).astype(BF).reshape(misfit.shape)

    @pl.loop(0, groups)
    def _(g):
        first = group_at(g)
        chosen(misfit[...].reshape(cl * exc, leaf), lslot, target_row(first), abuf, first)
        each(first, lambda t: a_copy(t).start())

    ain[me] = abuf[me]

    back[...] = jnp.zeros(back.shape, F32)

    @pl.loop(0, nears // NEAR_GROUP)
    def _(g):
        ins = [
            stacked(misfit[nrows[g * NEAR_GROUP + k]], ncols[g * NEAR_GROUP + k], cl + 2)
            for k in range(NEAR_GROUP)
        ]
        blocks = near[pl.ds(g * NEAR_GROUP, NEAR_GROUP)].reshape(NEAR_GROUP * leaf, leaf)
        back[...] += dot(jnp.concatenate(ins, axis=1), blocks, 1, 0)

    rimbuf[0] = back[:exc].astype(BF)
    rimbuf[1] = back[(cl + 1) * exc :].astype(BF)
    rim_left = send(rimbuf.at[0], rimin.at[1], b_send.at[0], b_recv.at[0], left)
    rim_right = send(rimbuf.at[1], rimin.at[0], b_send.at[1], b_recv.at[1], right)

    @pl.when(me > 0)
    def _():
        rim_left.start()

    @pl.when(me < n - 1)
    def _():
        rim_right.start()

    inner = pl.ds(exc, cl * exc)

    @pl.loop(0, groups)
    def _(g):
        first = group_at(groups - g)
        each(first, lambda t: a_arrival(t).wait_recv())
        back[inner, :] += expanded(ain, owner_row(first), rin, first)

    @pl.when(me < n - 1)
    def _():
        rim_left.wait_recv()
        back[pl.ds(cl * exc, exc), :] += rimin[1].astype(F32)

    @pl.when(me > 0)
    def _():
        rim_right.wait_recv()
        back[pl.ds(exc, exc), :] += rimin[0].astype(F32)

    def flat(value):
        return jnp.concatenate([value[c * exc : (c + 1) * exc] for c in range(cl)], axis=1)

    full = flat(back[inner, :])
    high = full.astype(BF)
    rest = full - high.astype(F32)
    mid = rest.astype(BF)
    low = (rest - mid.astype(F32)).astype(BF)
    parts[...] = jnp.concatenate([high, mid, flat(field[...]).astype(BF), low], axis=0)

    @pl.loop(0, groups)
    def _(g):
        first = group_at(g)
        each(first, lambda t: r_copy(t).wait_send())
        each(first, lambda t: c_copy(t).wait_send())
        each(first, lambda t: a_copy(t).wait_send())

    @pl.when(me > 0)
    def _():
        to_left.wait_send()
        rim_left.wait_send()

    @pl.when(me < n - 1)
    def _():
        to_right.wait_send()
        rim_right.wait_send()


def unsort(order, parts, pot, grad):
    exc, panels = pot.shape
    spot = jnp.transpose(jnp.broadcast_to(order[...].astype(F32), (8, panels)))[:, :1]
    lanes = lax.broadcasted_iota(jnp.int32, (panels, panels), 1).astype(F32)
    inverse = (lanes == spot).astype(F32).astype(BF)
    result = dot(parts[...], inverse, 1, 0)
    pot[...] = result[2 * exc : 3 * exc].astype(BF)
    grad[...] = (result[exc : 2 * exc] + result[3 * exc :]) + result[:exc]


def shards(
    charges,
    targets,
    panel_order,
    near_blocks,
    near_rows,
    near_cols,
    far_left,
    far_right,
    far_rows,
    far_slot,
    far_table,
):
    n = lax.axis_size("rows")
    panels, exc = charges.shape
    nears, leaf, _ = near_blocks.shape
    fars, _, rank = far_left.shape
    cl = panels // leaf
    wide = far_table.shape[1] // n * rank
    vmem = pl.BlockSpec(memory_space=pltpu.VMEM)
    smem = pl.BlockSpec(memory_space=pltpu.SMEM)
    anywhere = pl.BlockSpec(memory_space=pl.ANY)
    sems = pltpu.SemaphoreType.DMA((n,))
    pair = pltpu.SemaphoreType.DMA((2,))
    parts = pl.pallas_call(
        functools.partial(kernel, n),
        out_shape=jax.ShapeDtypeStruct((4 * exc, panels), BF),
        in_specs=[vmem, vmem, vmem, anywhere, smem, smem, vmem, vmem, smem, smem, smem],
        out_specs=vmem,
        scratch_shapes=[
            pltpu.VMEM((nears, leaf, leaf), BF),
            pltpu.VMEM((panels, panels), BF),
            pltpu.VMEM((cl + 2, exc, leaf), BF),
            pltpu.VMEM((cl * exc, leaf), F32),
            pltpu.VMEM((fars * rank, 2 * leaf), BF),
            pltpu.VMEM((1, fars * rank), jnp.int32),
            pltpu.VMEM((n, wide, leaf), BF),
            pltpu.VMEM((n, wide, leaf), BF),
            pltpu.VMEM((n, wide, leaf), BF),
            pltpu.VMEM((n, exc, wide), BF),
            pltpu.VMEM((n, exc, wide), BF),
            pltpu.VMEM((n, exc, wide), BF),
            pltpu.VMEM((n, exc, wide), BF),
            pltpu.VMEM((cl * exc, leaf), F32),
            pltpu.VMEM((cl, exc, leaf), BF),
            pltpu.VMEM(((cl + 2) * exc, leaf), F32),
            pltpu.VMEM((2, exc, leaf), BF),
            pltpu.VMEM((2, exc, leaf), BF),
            pltpu.VMEM((n // GROUP, GROUP, wide), jnp.int32),
            pltpu.SemaphoreType.DMA,
            sems,
            sems,
            sems,
            sems,
            sems,
            sems,
            pair,
            pair,
            pair,
            pair,
        ],
        compiler_params=pltpu.CompilerParams(
            collective_id=0, has_side_effects=True, vmem_limit_bytes=56 * 2**20
        ),
    )(
        charges.T,
        targets.T,
        panel_order,
        near_blocks,
        near_rows,
        near_cols,
        far_left.transpose(0, 2, 1),
        far_right.transpose(0, 2, 1),
        far_rows,
        far_slot,
        far_table,
    )
    potentials, gradient = pl.pallas_call(
        unsort,
        out_shape=(
            jax.ShapeDtypeStruct((exc, panels), BF),
            jax.ShapeDtypeStruct((exc, panels), F32),
        ),
        in_specs=[vmem, vmem],
        out_specs=(vmem, vmem),
        compiler_params=pltpu.CompilerParams(vmem_limit_bytes=32 * 2**20),
    )(panel_order, parts)
    return potentials.T, gradient.T


def solution(mesh):
    in_specs = (
        P(("groups", "rows"), None),
        P(("groups", "rows"), None),
        P(("groups", "rows"), None),
        P(("groups", "rows"), None, None),
        P(("groups", "rows")),
        P(("groups", "rows")),
        P(("groups", "rows"), None, None),
        P(("groups", "rows"), None, None),
        P(("groups", "rows")),
        P(("groups", "rows")),
        P(("groups", "rows"), None),
    )
    out_specs = (P(("groups", "rows"), None), P(("groups", "rows"), None))
    return jax.shard_map(shards, mesh=mesh, in_specs=in_specs, out_specs=out_specs, check_vma=False)
```

```python
import functools

import jax
import jax.numpy as jnp
from jax import lax
from jax.experimental import pallas as pl
from jax.experimental.pallas import tpu as pltpu
from jax.sharding import PartitionSpec as P

BF = jnp.bfloat16
F32 = jnp.float32
GROUP = 4
NEAR_GROUP = 32


def dot(a, b, ca, cb):
    return lax.dot_general(a, b, (((ca,), (cb,)), ((), ())), preferred_element_type=F32)


def kernel(
    n,
    charges,
    targets,
    order,
    near_hbm,
    nrows,
    ncols,
    fleft,
    fright,
    frows,
    fslot,
    ftable,
    parts,
    near,
    pt,
    ext,
    want,
    factors,
    target,
    rslot,
    rin,
    lslot,
    cbuf,
    cin,
    abuf,
    ain,
    field,
    misfit,
    back,
    rimbuf,
    rimin,
    rowtab,
    near_sem,
    r_send,
    r_recv,
    c_send,
    c_recv,
    a_send,
    a_recv,
    e_send,
    e_recv,
    b_send,
    b_recv,
):
    me = lax.axis_index("rows")
    left, right = me - 1, me + 1
    exc, panels = charges.shape
    nears, leaf, _ = near.shape
    fars, rank, _ = fleft.shape
    cap = ftable.shape[1] // n
    cl = panels // leaf
    wide = cap * rank

    near_copy = pltpu.make_async_copy(near_hbm, near, near_sem)
    near_copy.start()
    barrier = pltpu.get_barrier_semaphore()

    @pl.loop(1, n)
    def _(d):
        pl.semaphore_signal(
            barrier,
            inc=1,
            device_id={"rows": lax.rem(me + d, n)},
            device_id_type=pl.DeviceIdType.MESH,
        )

    lane_slot = lax.broadcasted_iota(jnp.int32, (1, wide), 1) // rank
    factors[:, :leaf] = fright[...].reshape(fars * rank, leaf)
    factors[:, leaf:] = fleft[...].reshape(fars * rank, leaf)
    for b in range(fars):
        rank_lane = lax.broadcasted_iota(jnp.int32, (1, rank), 1)
        target[:, b * rank : (b + 1) * rank] = fslot[b] * rank + rank_lane

    def send(src, dst, send_sem, recv_sem, d):
        return pltpu.make_async_remote_copy(
            src_ref=src,
            dst_ref=dst,
            send_sem=send_sem,
            recv_sem=recv_sem,
            device_id={"rows": d},
            device_id_type=pl.DeviceIdType.MESH,
        )

    @pl.loop(0, n // GROUP)
    def _(g):
        shape = (GROUP * wide, fars * rank)
        hot = lax.broadcasted_iota(jnp.int32, shape, 0) + g * (GROUP * wide) == target[...]
        placed = dot(hot.astype(F32).astype(BF), factors[...], 1, 0).astype(BF)
        rslot[pl.ds(g * GROUP, GROUP)] = placed[:, :leaf].reshape(GROUP, wide, leaf)
        lslot[pl.ds(g * GROUP, GROUP)] = placed[:, leaf:].reshape(GROUP, wide, leaf)

    rin[me] = rslot[me]
    pt[...] = (
        lax.broadcasted_iota(jnp.int32, (panels, panels), 0) == order[...]
    ).astype(F32).astype(BF)
    both = jnp.concatenate([charges[...], targets[...]], axis=0)
    sorted_t = dot(both, pt[...], 1, 0).astype(BF)
    for c in range(cl):
        ext[c + 1] = sorted_t[:exc, c * leaf : (c + 1) * leaf]
        want[pl.ds(c * exc, exc), :] = sorted_t[exc:, c * leaf : (c + 1) * leaf].astype(F32)

    pl.semaphore_wait(barrier, n - 1)

    groups = n // GROUP

    def each(first, act):
        for k in range(GROUP):
            other = first + lax.rem(me + k, GROUP)

            @pl.when(other != me)
            def _():
                act(other)

    def group_at(g):
        return lax.rem(me // GROUP + g, groups) * GROUP

    def r_copy(t):
        return send(rslot.at[t], rin.at[me], r_send.at[t], r_recv.at[me], t)

    def r_arrival(t):
        return send(rslot.at[me], rin.at[t], r_send.at[t], r_recv.at[t], t)

    def c_copy(t):
        return send(cbuf.at[t], cin.at[me], c_send.at[t], c_recv.at[me], t)

    def c_arrival(t):
        return send(cbuf.at[t], cin.at[t], c_send.at[t], c_recv.at[t], t)

    def a_copy(t):
        return send(abuf.at[t], ain.at[me], a_send.at[t], a_recv.at[me], t)

    def a_arrival(t):
        return send(abuf.at[t], ain.at[t], a_send.at[t], a_recv.at[t], t)

    @pl.loop(0, groups)
    def _(g):
        each(group_at(g), lambda t: r_copy(t).start())

    to_left = send(ext.at[1], ext.at[cl + 1], e_send.at[0], e_recv.at[0], left)
    to_right = send(ext.at[cl], ext.at[0], e_send.at[1], e_recv.at[1], right)

    @pl.when(me > 0)
    def _():
        to_left.start()

    @pl.when(me < n - 1)
    def _():
        to_right.start()

    @pl.loop(0, n)
    def _(s):
        slots = lane_slot + s * cap

        def some(g, acc):
            for k in range(16):
                b = g * 16 + k
                acc = jnp.where(slots == fslot[b], frows[b], acc)
            return acc

        rowtab[s // GROUP, pl.ds(lax.rem(s, GROUP), 1)] = lax.fori_loop(0, fars // 16, some, jnp.zeros((1, wide), jnp.int32))

    @pl.when(me < n - 1)
    def _():
        to_left.wait_recv()

    @pl.when(me == n - 1)
    def _():
        ext[cl + 1] = jnp.zeros((exc, leaf), BF)

    @pl.when(me > 0)
    def _():
        to_right.wait_recv()

    @pl.when(me == 0)
    def _():
        ext[0] = jnp.zeros((exc, leaf), BF)

    near_copy.wait()
    nothing = jnp.zeros((exc, leaf), BF)

    def stacked(value, place_of, count):
        return jnp.concatenate(
            [lax.select(place_of == r, value, nothing) for r in range(count)], axis=0
        )

    field[...] = jnp.zeros(field.shape, F32)

    @pl.loop(0, nears // NEAR_GROUP)
    def _(g):
        ins, blocks = [], []
        for k in range(NEAR_GROUP):
            b = g * NEAR_GROUP + k
            ins.append(stacked(ext[ncols[b]], nrows[b], cl))
            blocks.append(near[b])
        field[...] += dot(jnp.concatenate(ins, axis=1), jnp.concatenate(blocks, axis=1), 1, 1)

    def owner_row(first):
        rows = []
        for t in range(GROUP):
            row = jnp.full((1, wide), -1, jnp.int32)
            for k in range(cap):
                row = jnp.where(lane_slot == k, ftable[0, (first + t) * cap + k], row)
            rows.append(row)
        return jnp.concatenate(rows, axis=1)

    def target_row(first):
        return jnp.concatenate([rowtab[first // GROUP, t : t + 1] for t in range(GROUP)], axis=1)

    def chosen(value, factor, row, out, first):
        product = dot(value, factor[pl.ds(first, GROUP)].reshape(GROUP * wide, leaf), 1, 1)
        total = jnp.zeros((exc, GROUP * wide), F32)
        for c in range(cl):
            total = total + jnp.where(row == c, product[c * exc : (c + 1) * exc], 0.0)
        total = total.astype(BF)
        for t in range(GROUP):
            out[first + t] = total[:, t * wide : (t + 1) * wide]

    def expanded(value, row, factor, first):
        parts = jnp.concatenate([value[first + t] for t in range(GROUP)], axis=1)
        masks = [(row == c).astype(F32).astype(BF) for c in range(cl)]
        spread = jnp.concatenate([parts * mask for mask in masks], axis=0)
        return dot(spread, factor[pl.ds(first, GROUP)].reshape(GROUP * wide, leaf), 1, 0)

    mine = ext[1 : cl + 1].reshape(cl * exc, leaf)

    @pl.loop(0, groups)
    def _(g):
        first = group_at(groups - g)
        each(first, lambda t: r_arrival(t).wait_recv())
        chosen(mine, rin, owner_row(first), cbuf, first)
        each(first, lambda t: c_copy(t).start())

    cin[me] = cbuf[me]

    @pl.loop(0, groups)
    def _(g):
        first = group_at(g)
        each(first, lambda t: c_arrival(t).wait_recv())
        field[...] += expanded(cin, target_row(first), lslot, first)

    misfit[...] = (field[...] - want[...]).astype(BF).reshape(misfit.shape)

    @pl.loop(0, groups)
    def _(g):
        first = group_at(g)
        chosen(misfit[...].reshape(cl * exc, leaf), lslot, target_row(first), abuf, first)
        each(first, lambda t: a_copy(t).start())

    ain[me] = abuf[me]

    back[...] = jnp.zeros(back.shape, F32)

    @pl.loop(0, nears // NEAR_GROUP)
    def _(g):
        ins = [
            stacked(misfit[nrows[g * NEAR_GROUP + k]], ncols[g * NEAR_GROUP + k], cl + 2)
            for k in range(NEAR_GROUP)
        ]
        blocks = near[pl.ds(g * NEAR_GROUP, NEAR_GROUP)].reshape(NEAR_GROUP * leaf, leaf)
        back[...] += dot(jnp.concatenate(ins, axis=1), blocks, 1, 0)

    rimbuf[0] = back[:exc].astype(BF)
    rimbuf[1] = back[(cl + 1) * exc :].astype(BF)
    rim_left = send(rimbuf.at[0], rimin.at[1], b_send.at[0], b_recv.at[0], left)
    rim_right = send(rimbuf.at[1], rimin.at[0], b_send.at[1], b_recv.at[1], right)

    @pl.when(me > 0)
    def _():
        rim_left.start()

    @pl.when(me < n - 1)
    def _():
        rim_right.start()

    inner = pl.ds(exc, cl * exc)

    @pl.loop(0, groups)
    def _(g):
        first = group_at(groups - g)
        each(first, lambda t: a_arrival(t).wait_recv())
        back[inner, :] += expanded(ain, owner_row(first), rin, first)

    @pl.when(me < n - 1)
    def _():
        rim_left.wait_recv()
        back[pl.ds(cl * exc, exc), :] += rimin[1].astype(F32)

    @pl.when(me > 0)
    def _():
        rim_right.wait_recv()
        back[pl.ds(exc, exc), :] += rimin[0].astype(F32)

    def flat(value):
        return jnp.concatenate([value[c * exc : (c + 1) * exc] for c in range(cl)], axis=1)

    full = flat(back[inner, :])
    high = full.astype(BF)
    rest = full - high.astype(F32)
    mid = rest.astype(BF)
    low = (rest - mid.astype(F32)).astype(BF)
    parts[...] = jnp.concatenate([high, mid, flat(field[...]).astype(BF), low], axis=0)

    @pl.loop(0, groups)
    def _(g):
        first = group_at(g)
        each(first, lambda t: r_copy(t).wait_send())
        each(first, lambda t: c_copy(t).wait_send())
        each(first, lambda t: a_copy(t).wait_send())

    @pl.when(me > 0)
    def _():
        to_left.wait_send()
        rim_left.wait_send()

    @pl.when(me < n - 1)
    def _():
        to_right.wait_send()
        rim_right.wait_send()


def unsort(order, parts, pot, grad):
    exc, panels = pot.shape
    spot = jnp.transpose(jnp.broadcast_to(order[...].astype(F32), (8, panels)))[:, :1]
    lanes = lax.broadcasted_iota(jnp.int32, (panels, panels), 1).astype(F32)
    inverse = (lanes == spot).astype(F32).astype(BF)
    result = dot(parts[...], inverse, 1, 0)
    pot[...] = result[2 * exc : 3 * exc].astype(BF)
    grad[...] = (result[exc : 2 * exc] + result[3 * exc :]) + result[:exc]


def shards(
    charges,
    targets,
    panel_order,
    near_blocks,
    near_rows,
    near_cols,
    far_left,
    far_right,
    far_rows,
    far_slot,
    far_table,
):
    n = lax.axis_size("rows")
    panels, exc = charges.shape
    nears, leaf, _ = near_blocks.shape
    fars, _, rank = far_left.shape
    cl = panels // leaf
    wide = far_table.shape[1] // n * rank
    vmem = pl.BlockSpec(memory_space=pltpu.VMEM)
    smem = pl.BlockSpec(memory_space=pltpu.SMEM)
    anywhere = pl.BlockSpec(memory_space=pl.ANY)
    sems = pltpu.SemaphoreType.DMA((n,))
    pair = pltpu.SemaphoreType.DMA((2,))
    parts = pl.pallas_call(
        functools.partial(kernel, n),
        out_shape=jax.ShapeDtypeStruct((4 * exc, panels), BF),
        in_specs=[vmem, vmem, vmem, anywhere, smem, smem, vmem, vmem, smem, smem, smem],
        out_specs=vmem,
        scratch_shapes=[
            pltpu.VMEM((nears, leaf, leaf), BF),
            pltpu.VMEM((panels, panels), BF),
            pltpu.VMEM((cl + 2, exc, leaf), BF),
            pltpu.VMEM((cl * exc, leaf), F32),
            pltpu.VMEM((fars * rank, 2 * leaf), BF),
            pltpu.VMEM((1, fars * rank), jnp.int32),
            pltpu.VMEM((n, wide, leaf), BF),
            pltpu.VMEM((n, wide, leaf), BF),
            pltpu.VMEM((n, wide, leaf), BF),
            pltpu.VMEM((n, exc, wide), BF),
            pltpu.VMEM((n, exc, wide), BF),
            pltpu.VMEM((n, exc, wide), BF),
            pltpu.VMEM((n, exc, wide), BF),
            pltpu.VMEM((cl * exc, leaf), F32),
            pltpu.VMEM((cl, exc, leaf), BF),
            pltpu.VMEM(((cl + 2) * exc, leaf), F32),
            pltpu.VMEM((2, exc, leaf), BF),
            pltpu.VMEM((2, exc, leaf), BF),
            pltpu.VMEM((n // GROUP, GROUP, wide), jnp.int32),
            pltpu.SemaphoreType.DMA,
            sems,
            sems,
            sems,
            sems,
            sems,
            sems,
            pair,
            pair,
            pair,
            pair,
        ],
        compiler_params=pltpu.CompilerParams(
            collective_id=0, has_side_effects=True, vmem_limit_bytes=56 * 2**20
        ),
    )(
        charges.T,
        targets.T,
        panel_order,
        near_blocks,
        near_rows,
        near_cols,
        far_left.transpose(0, 2, 1),
        far_right.transpose(0, 2, 1),
        far_rows,
        far_slot,
        far_table,
    )
    potentials, gradient = pl.pallas_call(
        unsort,
        out_shape=(
            jax.ShapeDtypeStruct((exc, panels), BF),
            jax.ShapeDtypeStruct((exc, panels), F32),
        ),
        in_specs=[vmem, vmem],
        out_specs=(vmem, vmem),
        compiler_params=pltpu.CompilerParams(vmem_limit_bytes=32 * 2**20),
    )(panel_order, parts)
    return potentials.T, gradient.T


def solution(mesh):
    in_specs = (
        P(("groups", "rows"), None),
        P(("groups", "rows"), None),
        P(("groups", "rows"), None),
        P(("groups", "rows"), None, None),
        P(("groups", "rows")),
        P(("groups", "rows")),
        P(("groups", "rows"), None, None),
        P(("groups", "rows"), None, None),
        P(("groups", "rows")),
        P(("groups", "rows")),
        P(("groups", "rows"), None),
    )
    out_specs = (P(("groups", "rows"), None), P(("groups", "rows"), None))
    return jax.shard_map(shards, mesh=mesh, in_specs=in_specs, out_specs=out_specs, check_vma=False)
```
